128 devices in a mesh: dp: 64 (over z, x_lo, y, core), tp: 2 (over x_hi).
Axes of the slice: x: 4 (x_hi: 2, x_lo: 2; x = x_hi * 2 + x_lo), y: 4, z: 4, core: 2. Of those that a mesh axis runs over, the one named last changes fastest.
Arguments:
- latents: bfloat16 [64, 256, 1024], P('dp', 'tp'), may hold values from -6 to 6
- conditioning: bfloat16 [64, 1024], P('dp'), may hold values from -6 to 6
- cotangent: bfloat16 [64, 256, 1024], P('dp', 'tp'), may hold values from -6 to 6
- modulate_weight: bfloat16 [1024, 1, 6144], P('dp'), may hold values from -0.1875 to 0.1875
- modulate_bias: bfloat16 [1, 6144], replicated, may hold values from -3 to 3
- attend_weight: bfloat16 [1, 1024, 3, 1024], P(None, 'dp', None, 'tp'), may hold values from -0.1875 to 0.1875
- attend_bias: bfloat16 [1, 2, 1024], P(None, None, 'tp'), may hold values from -2 to 2
- project_weight: bfloat16 [1, 1024, 1024], P(None, 'dp', 'tp'), may hold values from -1.5 to 1.5
- project_bias: bfloat16 [1, 1024], replicated, may hold values from -2 to 2
- hidden_weight: bfloat16 [1, 1024, 4096], P(None, 'dp', 'tp'), may hold values from -0.1875 to 0.1875
- hidden_bias: bfloat16 [1, 4096], P(None, 'tp'), may hold values from -2 to 2
- output_weight: bfloat16 [1, 1024, 4096], P(None, 'dp', 'tp'), may hold values from -0.09375 to 0.09375
- output_bias: bfloat16 [1, 1024], replicated, may hold values from -2 to 2
Outputs:
- block_output: bfloat16 [64, 256, 1024], P('dp', 'tp')
- grad_latents: bfloat16 [64, 256, 1024], P('dp', 'tp')
- grad_conditioning: bfloat16 [64, 1024], P('dp')
- grad_modulate_weight: float32 [1024, 1, 6144], P('dp')
- grad_modulate_bias: float32 [1, 6144], replicated
- grad_attend_weight: float32 [1, 1024, 3, 1024], P(None, 'dp', None, 'tp')
- grad_attend_bias: float32 [1, 2, 1024], P(None, None, 'tp')
- grad_project_weight: float32 [1, 1024, 1024], P(None, 'dp', 'tp')
- grad_project_bias: float32 [1, 1024], replicated
- grad_hidden_weight: float32 [1, 1024, 4096], P(None, 'dp', 'tp')
- grad_hidden_bias: float32 [1, 4096], P(None, 'tp')
- grad_output_weight: float32 [1, 1024, 4096], P(None, 'dp', 'tp')
- grad_output_bias: float32 [1, 1024], replicated
The draws below stay inside these ranges and needn't reach their ends.
All inputs are finite; a program needn't handle non-finite values.
Results may differ from the reference program's by a relative error of at most 0.01615.
The reference program's roundings to bfloat16 on the way count: a program that leaves them out, or rounds other values in their place, can miss the bound.
Values may be sent and summed in bfloat16 or wider, within the bound.
No kernel may reach another device: no remote copies, remote signals or barrier semaphores. Data moves between devices by JAX's collectives and lax.ppermute only.
A program may use at most 128 MiB of HBM per device.

```python
import math
import jax
import jax.numpy as jnp
from jax import lax

D = 1024
HEADS = 16
HEAD_DIM = 64
FF = 4096
LAYERS = 1
SEQ = 256
LATENTS = 64


def levels(key, dims, cuts, least, high):
    def one(dim, shards_of):
        draws = jax.random.uniform(jax.random.fold_in(jax.random.fold_in(key, 6), dim), (shards_of,), jnp.float32, least / len(cuts), high / len(cuts))
        return jnp.repeat(jnp.exp(draws), dims[dim] // shards_of).reshape((-1,) + (1,) * (len(dims) - dim - 1))

    gain = one(*cuts[0])
    for cut in cuts[1:]:
        gain = gain * one(*cut)
    return gain


def centred(rng, shape, spread, bound, cuts=(), kind=jnp.bfloat16):
    array = spread * jax.random.normal(rng, shape, jnp.float32)
    if cuts:
        array = array * levels(rng, shape, cuts, -0.22, 0.18)
    return jnp.clip(array, -bound, bound).astype(kind)


def setup_inputs(seed: int = 0) -> dict:
    arg_keys = jax.random.split(jax.random.key(seed), 14)
    return {
        "latents": centred(arg_keys[0], (LATENTS, SEQ, D), 1.0, 6.0, ((0, 64), (1, 2))),
        "conditioning": centred(arg_keys[1], (LATENTS, D), 1.0, 6.0, ((0, 64),)),
        "cotangent": centred(arg_keys[2], (LATENTS, SEQ, D), 1.0, 6.0, ((0, 64), (1, 2))),
        "modulate_weight": centred(arg_keys[3], (D, LAYERS, 6 * D), D ** -0.5, 0.1875, ((0, 64),)),
        "modulate_bias": centred(arg_keys[4], (LAYERS, 6 * D), 0.5, 3.0),
        "attend_weight": centred(arg_keys[5], (LAYERS, D, 3, D), D ** -0.5, 0.1875, ((1, 64), (3, 2))),
        "attend_bias": centred(arg_keys[6], (LAYERS, 2, D), 0.3, 2.0, ((2, 2),)),
        "project_weight": centred(arg_keys[7], (LAYERS, D, D), (max(D // 64, 1)) ** -0.5, 1.5, ((1, 64), (2, 2))),
        "project_bias": centred(arg_keys[8], (LAYERS, D), 0.3, 2.0),
        "hidden_weight": centred(arg_keys[9], (LAYERS, D, FF), D ** -0.5, 0.1875, ((1, 64), (2, 2))),
        "hidden_bias": centred(arg_keys[10], (LAYERS, FF), 0.3, 2.0, ((1, 2),)),
        "output_weight": centred(arg_keys[11], (LAYERS, D, FF), FF ** -0.5, 0.09375, ((1, 64), (2, 2))),
        "output_bias": centred(arg_keys[12], (LAYERS, D), 0.3, 2.0),
    }


HIGH = lax.Precision.HIGHEST

@jax.custom_vjp
def low(v):
    return lax.optimization_barrier(v.astype(jnp.bfloat16)).astype(jnp.float32)

@jax.custom_vjp
def low_back(v):
    return v

def low_keep(v):
    return (low(v), None)

def low_pass(kept, grad):
    return (grad,)

def back_keep(v):
    return (v, None)

def back_low(kept, grad):
    return (low(grad),)
low.defvjp(low_keep, low_pass)
low_back.defvjp(back_keep, back_low)

def layer_norm(values):
    centered = values - lax.optimization_barrier(jnp.mean(values, axis=-1, keepdims=True))
    return centered * lax.rsqrt(lax.optimization_barrier(jnp.mean(centered * centered, axis=-1, keepdims=True)) + 1e-06)

def rounded_both(values):
    return low(low_back(values))

def layer_step(hidden, group_mods, weights, layer_index):
    attend_weight, attend_bias, project_weight, project_bias, hidden_weight, hidden_bias, output_weight, output_bias = weights
    shift_first = group_mods[:, 0][:, None, :]
    scale_first = group_mods[:, 1][:, None, :]
    gate_first = group_mods[:, 2][:, None, :]
    shift_second = group_mods[:, 3][:, None, :]
    scale_second = group_mods[:, 4][:, None, :]
    gate_second = group_mods[:, 5][:, None, :]
    groups = hidden.shape[0]
    length = hidden.shape[1]
    first = low(layer_norm(hidden) * (1.0 + scale_first) + shift_first)
    packed = jnp.einsum('gsd,dte->tgse', first, attend_weight[layer_index], precision=HIGH)
    query = rounded_both(packed[0] + attend_bias[layer_index, 0])
    key = rounded_both(packed[1])
    value = rounded_both(packed[2] + attend_bias[layer_index, 1])
    shape = (groups, length, HEADS, HEAD_DIM)
    scores = jnp.einsum('gqhe,gkhe->ghqk', query.reshape(shape), key.reshape(shape), precision=HIGH) * HEAD_DIM ** (-0.5)
    scores = low_back(scores)
    probs = low(jax.nn.softmax(scores, axis=-1))
    mixed = jnp.einsum('ghqk,gkhe->gqhe', probs, value.reshape(shape), precision=HIGH).reshape(groups, length, D)
    mixed = rounded_both(mixed)
    projected = low_back(jnp.einsum('gsi,oi->gso', mixed, project_weight[layer_index], precision=HIGH) + project_bias[layer_index])
    middle = hidden + gate_first * projected
    second = low(layer_norm(middle) * (1.0 + scale_second) + shift_second)
    pre = low_back(jnp.einsum('gsd,df->gsf', second, hidden_weight[layer_index], precision=HIGH) + hidden_bias[layer_index])
    active = low(jax.nn.gelu(pre, approximate=True))
    branch = low_back(jnp.einsum('gsf,of->gso', active, output_weight[layer_index], precision=HIGH) + output_bias[layer_index])
    return middle + gate_second * branch

def stack_layers(hidden, group_mods, weights):
    for layer_index in range(LAYERS):
        hidden = layer_step(hidden, group_mods[layer_index], weights, layer_index)
    return hidden

def forward(latents, conditioning, modulate_weight, modulate_bias, attend_weight, attend_bias, project_weight, project_bias, hidden_weight, hidden_bias, output_weight, output_bias):
    weights = (attend_weight, attend_bias, project_weight, project_bias, hidden_weight, hidden_bias, output_weight, output_bias)
    silu_low = low(jax.nn.silu(conditioning))
    modulations = jnp.einsum('nd,dlm->lnm', silu_low, modulate_weight, precision=HIGH) + modulate_bias[:, None, :]
    modulations = low_back(modulations).reshape(LAYERS, LATENTS, 6, D)
    group = math.gcd(LATENTS, max(1, 4096 // SEQ))
    count = LATENTS // group
    stacked = latents.reshape(count, group, SEQ, D)
    grouped = modulations.reshape(LAYERS, count, group, 6, D).transpose(1, 0, 2, 3, 4)
    step_fn = jax.checkpoint(lambda pair: stack_layers(pair[0], pair[1], weights))
    return lax.map(step_fn, (stacked, grouped)).reshape(LATENTS, SEQ, D)

def reference(latents, conditioning, cotangent, modulate_weight, modulate_bias, attend_weight, attend_bias, project_weight, project_bias, hidden_weight, hidden_bias, output_weight, output_bias):
    inputs = (latents, conditioning, modulate_weight, modulate_bias, attend_weight, attend_bias, project_weight, project_bias, hidden_weight, hidden_bias, output_weight, output_bias)
    floats = tuple((item.astype(jnp.float32) for item in inputs))
    result, pullback = jax.vjp(forward, *floats)
    grads = pullback(cotangent.astype(jnp.float32))
    return (result.astype(jnp.bfloat16), grads[0].astype(jnp.bfloat16), grads[1].astype(jnp.bfloat16), grads[2], grads[3], grads[4], grads[5], grads[6], grads[7], grads[8], grads[9], grads[10], grads[11])
```

```python
import jax
import jax.numpy as jnp
from jax import lax
from jax.sharding import Mesh
from jax.sharding import PartitionSpec as P

HEAD_DIM = 64
EPS = 1e-06
F32 = jnp.float32
BF16 = jnp.bfloat16
DP = ("z", "w", "y", "c")
CHIPS = ("z", "w", "y", "t")


def normalize(values):
    centered = values - jnp.mean(values, axis=-1, keepdims=True)
    inverse = lax.rsqrt(jnp.mean(centered * centered, axis=-1, keepdims=True) + EPS)
    return (centered * inverse, inverse)


def normalize_back(grad, normed, inverse):
    return inverse * (
        grad
        - jnp.mean(grad, axis=-1, keepdims=True)
        - normed * jnp.mean(grad * normed, axis=-1, keepdims=True)
    )


def dot(left, right):
    return jnp.dot(left, right, preferred_element_type=F32)


def dot_nt(left, right):
    return lax.dot_general(left, right, (((1,), (1,)), ((), ())), preferred_element_type=F32)


def dot_tn(left, right):
    return lax.dot_general(left, right, (((0,), (0,)), ((), ())), preferred_element_type=F32)


def swap_core(piece):
    return lax.ppermute(piece, "c", [(0, 1), (1, 0)])


def swap_t(piece):
    return lax.ppermute(piece, "t", [(0, 1), (1, 0)])


def swap_layout(piece):
    return lax.ppermute(piece, ("c", "t"), [(0, 0), (1, 2), (2, 1), (3, 3)])


def shift_plane(piece, step, last):
    perm = []
    for z in range(4):
        for y in range(4):
            for c in range(2):
                along_z = (c == 0) == last
                z2, y2 = ((z + step) % 4, y) if along_z else (z, (y + step) % 4)
                perm.append(((z * 4 + y) * 2 + c, (z2 * 4 + y2) * 2 + c))
    return lax.ppermute(piece, ("z", "y", "c"), perm)


def shift_x(piece, step):
    def place(x):
        return (x % 2) * 2 + x // 2

    return lax.ppermute(piece, ("w", "t"), [(place(x), place((x + step) % 4)) for x in range(4)])


STEPS = (2, 1, 3)


class Place:
    def __init__(self):
        self.z = lax.axis_index("z")
        self.w = lax.axis_index("w")
        self.y = lax.axis_index("y")
        self.c = lax.axis_index("c")
        self.t = lax.axis_index("t")
        self.x = self.t * 2 + self.w
        first = self.c == 0
        self.last = jnp.where(first, self.z, self.y)
        self.before = jnp.where(first, self.y, self.z)
        self.first = first

    def zy(self, last, before):
        return (jnp.where(self.first, last, before), jnp.where(self.first, before, last))


def gather_attention(piece, place):
    rows, width = piece.shape
    got = [(0, piece)] + [(k, shift_x(piece, -k)) for k in STEPS]
    buffer = jnp.zeros((2, 2, rows, width), piece.dtype)
    for k, block in got:
        x = (place.x + k) % 4
        buffer = lax.dynamic_update_slice(buffer, block[None, None], (x // 2, x % 2, 0, 0))
    got = [(0, buffer)] + [(k, shift_plane(buffer, -k, False)) for k in STEPS]
    middle = jnp.zeros((4,) + buffer.shape, piece.dtype)
    for k, block in got:
        middle = lax.dynamic_update_slice(middle, block[None], ((place.before + k) % 4, 0, 0, 0, 0))
    got = [(0, middle)] + [(k, shift_plane(middle, -k, True)) for k in STEPS]
    full = [jnp.zeros((2, 4, 2, 4, rows, n), piece.dtype) for n in (768, 256)]
    for k, block in got:
        last = (place.last + k) % 4
        for before in range(4):
            z, y = place.zy(last, before)
            part = block[before][:, None, :, None]
            full[0] = lax.dynamic_update_slice(full[0], part[..., :768], (0, z, 0, y, 0, 0))
            full[1] = lax.dynamic_update_slice(full[1], part[..., 768:], (0, z, 0, y, 0, 0))
    return full[0].reshape(2, 1024, 768), full[1].reshape(2, 1024, 256)


def add_up(own, received):
    total = own.astype(F32)
    for block in received:
        total = total + block.astype(F32)
    return total


def scatter_plane(pick, place):
    def group(k):
        last = (place.last + k) % 4
        return jnp.stack([pick(*place.zy(last, before)) for before in range(4)])

    received = [shift_plane(group(k), k, True) for k in STEPS]
    total = add_up(group(0), received).astype(BF16)

    def one(k):
        return lax.dynamic_index_in_dim(total, (place.before + k) % 4, 0, keepdims=False)

    received = [shift_plane(one(k), k, False) for k in STEPS]
    return add_up(one(0), received)


def scatter_attention(grads, place):
    width = grads.shape[-1]
    grads = grads.reshape(2, 4, 2, 4, 32, width)

    def pick(z, y):
        return lax.dynamic_slice(grads, (0, z, 0, y, 0, 0), (2, 1, 2, 1, 32, width)).reshape(
            2, 2, 32, width
        )

    total = scatter_plane(pick, place).astype(BF16)

    def one(k):
        x = (place.x + k) % 4
        return lax.dynamic_slice(total, (x // 2, x % 2, 0, 0), (1, 1, 32, width))[0, 0]

    received = [shift_x(one(k), k) for k in STEPS]
    return add_up(one(0), received)


def scatter_forward(grads, place):
    width = grads.shape[-1]
    grads = grads.reshape(2, 32, 2, 16, width)
    theirs = lax.dynamic_index_in_dim(grads, 1 - place.c, 2, keepdims=False)
    mine = lax.dynamic_index_in_dim(grads, place.c, 2, keepdims=False)
    both = add_up(mine, [swap_core(theirs)]).astype(BF16).reshape(2, 4, 2, 4, 16, width)

    def pick(z, y):
        return lax.dynamic_slice(both, (0, z, 0, y, 0, 0), (2, 1, 2, 1, 16, width)).reshape(
            2, 2, 16, width
        )

    total = scatter_plane(pick, place).astype(BF16)
    theirs = lax.dynamic_index_in_dim(total, 1 - place.w, 1, keepdims=False)
    mine = lax.dynamic_index_in_dim(total, place.w, 1, keepdims=False)
    return add_up(mine, [lax.ppermute(theirs, "w", [(0, 1), (1, 0)])])


def heads_of(flat):
    return flat.reshape(flat.shape[0], -1, HEAD_DIM)


def attention_forward(query, key, value):
    scale = HEAD_DIM ** (-0.5)
    scores = (
        jnp.einsum("qhe,khe->hqk", heads_of(query), heads_of(key), preferred_element_type=F32)
        * scale
    )
    highest = jnp.max(scores, axis=-1, keepdims=True)
    expd = jnp.exp(scores - highest)
    probs = expd / jnp.sum(expd, axis=-1, keepdims=True)
    mixed = jnp.einsum(
        "hqk,khe->qhe", probs.astype(BF16), heads_of(value), preferred_element_type=F32
    )
    return mixed.reshape(query.shape).astype(BF16), probs


def attention_backward(query, key, value, probs, grad_mixed):
    scale = HEAD_DIM ** (-0.5)
    shape = query.shape
    query, key, value, grad_mixed = (heads_of(item) for item in (query, key, value, grad_mixed))
    grad_value = jnp.einsum(
        "hqk,qhe->khe", probs.astype(BF16), grad_mixed, preferred_element_type=F32
    )
    grad_probs = jnp.einsum("qhe,khe->hqk", grad_mixed, value, preferred_element_type=F32)
    grad_scores = (
        probs * (grad_probs - jnp.sum(grad_probs * probs, axis=-1, keepdims=True))
    ).astype(BF16)
    grad_query = jnp.einsum("hqk,khe->qhe", grad_scores, key, preferred_element_type=F32) * scale
    grad_key = jnp.einsum("hqk,qhe->khe", grad_scores, query, preferred_element_type=F32) * scale
    return tuple(item.reshape(shape).astype(BF16) for item in (grad_query, grad_key, grad_value))


def halves(rows):
    half = rows.shape[0] // 2
    return rows[:half], rows[half:]


def shards(
    latents,
    conditioning,
    cotangent,
    modulate_weight,
    modulate_bias,
    attend_weight,
    attend_bias,
    project_weight,
    project_bias,
    hidden_weight,
    hidden_bias,
    output_weight,
    output_bias,
):
    place = Place()
    width = conditioning.shape[1]

    silu_rows = lax.all_to_all(conditioning.reshape(64, 16), DP, 0, 0, tiled=True)
    silu_rows = jax.nn.silu(silu_rows.astype(F32)).astype(BF16)
    modulate = modulate_weight[:, 0]

    quarters = jnp.concatenate(
        [attend_weight[0].reshape(16, 3, 2, 256), project_weight[0].reshape(16, 1, 2, 256)], axis=1
    )
    mine = lax.dynamic_index_in_dim(quarters, place.c, 2, keepdims=False).reshape(16, 1024)
    theirs = lax.dynamic_index_in_dim(quarters, 1 - place.c, 2, keepdims=False).reshape(16, 1024)
    theirs = swap_core(theirs)
    piece = jnp.where(
        place.first, jnp.concatenate([mine, theirs]), jnp.concatenate([theirs, mine])
    )
    attend_full, project_full = gather_attention(piece, place)

    forward_pair = jnp.stack([hidden_weight[0], output_weight[0]])
    forward_full = lax.all_gather(forward_pair, DP, axis=1, tiled=True)
    up_full, down_full = forward_full[0], forward_full[1]

    bias_own = lax.dynamic_slice_in_dim(attend_bias[0], place.c * 256, 256, 1)
    bias_other = swap_t(bias_own)
    on_first = place.t == 0
    bias_pair = jnp.concatenate(
        [jnp.where(on_first, bias_own, bias_other), jnp.where(on_first, bias_other, bias_own)],
        axis=1,
    ).astype(F32)

    silu_chip = lax.dynamic_index_in_dim(silu_rows.reshape(32, 2, 16), place.t, 1, keepdims=False)
    terms = dot(silu_chip, modulate).reshape(64, 3072)
    terms = lax.all_to_all(terms, DP, 0, 0, tiled=True)
    mods_half = jnp.sum(terms, axis=0)
    mods = lax.all_gather(mods_half, "c", axis=0, tiled=True) + modulate_bias[0].astype(F32)
    mods = mods.reshape(6, width)

    stream = swap_layout(latents[0]).astype(F32)
    grad = swap_layout(cotangent[0]).astype(F32)

    normed_first, inverse_first = normalize(stream)
    first_in = (normed_first * (1.0 + mods[1]) + mods[0]).astype(BF16)
    first_all = jnp.concatenate([first_in, swap_core(first_in)])
    packed = [dot(first_all, attend_full[t]) for t in range(2)]
    query, key, value = (
        jnp.concatenate([part[:, i * 256 : (i + 1) * 256] for part in packed], axis=1)
        for i in range(3)
    )
    query = (query + bias_pair[0]).astype(BF16)
    key = key.astype(BF16)
    value = (value + bias_pair[1]).astype(BF16)
    mixed, probs = attention_forward(query, key, value)
    mixed_t = (mixed[:, :256], mixed[:, 256:])
    partial = dot_nt(mixed_t[0], project_full[0]) + dot_nt(mixed_t[1], project_full[1])
    own, other = halves(partial)
    projected = (
        own + swap_core(other.astype(BF16)).astype(F32) + project_bias[0].astype(F32)
    )
    middle = stream + mods[2] * projected

    normed_second, inverse_second = normalize(middle)
    second_in = (normed_second * (1.0 + mods[4]) + mods[3]).astype(BF16)
    second_all = jnp.concatenate([second_in, swap_t(second_in)])
    grad_branch = (grad * mods[5]).astype(BF16)
    out_bias_part = jnp.sum(grad_branch.astype(F32), axis=0)
    branch_all = jnp.concatenate([grad_branch, swap_t(grad_branch)])
    pre = dot(second_all, up_full) + hidden_bias[0].astype(F32)
    active = jax.nn.gelu(pre, approximate=True).astype(BF16)
    own, other = halves(dot_nt(active, down_full))
    branch = own + swap_t(other.astype(BF16)).astype(F32) + output_bias[0].astype(F32)
    block_output = swap_layout((middle + mods[5] * branch).astype(BF16))[None]

    grad_gate_second = jnp.sum(grad * branch, axis=0)
    grad_down = dot_tn(branch_all, active).astype(BF16)
    grad_active = dot(branch_all, down_full)
    _, gelu_back = jax.vjp(lambda inner: jax.nn.gelu(inner, approximate=True), pre)
    grad_pre = gelu_back(grad_active)[0].astype(BF16)
    hidden_bias_part = jnp.sum(grad_pre.astype(F32), axis=0)
    own, other = halves(dot_nt(grad_pre, up_full))
    grad_second = own + swap_t(other.astype(BF16)).astype(F32)
    grad_up = dot_tn(second_all, grad_pre).astype(BF16)
    forward_grads = scatter_forward(jnp.stack([grad_up, grad_down]), place)
    grad_shift_second = jnp.sum(grad_second, axis=0)
    grad_scale_second = jnp.sum(grad_second * normed_second, axis=0)
    grad_middle = grad + normalize_back(
        grad_second * (1.0 + mods[4]), normed_second, inverse_second
    )

    grad_gate_first = jnp.sum(grad_middle * projected, axis=0)
    grad_projected = (grad_middle * mods[2]).astype(BF16)
    project_bias_part = jnp.sum(grad_projected.astype(F32), axis=0)
    projected_all = jnp.concatenate([grad_projected, swap_core(grad_projected)])
    grad_mixed = jnp.concatenate(
        [dot(projected_all, project_full[t]).astype(BF16) for t in range(2)], axis=1
    )
    grads = attention_backward(query, key, value, probs, grad_mixed)
    grad_packed = [
        jnp.concatenate([item[:, t * 256 : (t + 1) * 256] for item in grads], axis=1)
        for t in range(2)
    ]
    own, other = halves(
        dot_nt(grad_packed[0], attend_full[0]) + dot_nt(grad_packed[1], attend_full[1])
    )
    grad_first = own + swap_core(other.astype(BF16)).astype(F32)
    attention_grads = jnp.stack(
        [
            jnp.concatenate(
                [
                    dot_tn(first_all, grad_packed[t]).astype(BF16),
                    dot_tn(projected_all, mixed_t[t]).astype(BF16),
                ],
                axis=1,
            )
            for t in range(2)
        ]
    )
    attend_bias_part = jnp.stack(
        [
            jnp.stack([jnp.sum(grads[i][:, t * 256 : (t + 1) * 256].astype(F32), axis=0) for i in (0, 2)])
            for t in range(2)
        ]
    )
    grad_shift_first = jnp.sum(grad_first, axis=0)
    grad_scale_first = jnp.sum(grad_first * normed_first, axis=0)
    grad_stream = grad_middle + normalize_back(
        grad_first * (1.0 + mods[1]), normed_first, inverse_first
    )
    grad_latents = swap_layout(grad_stream.astype(BF16))[None]

    sums = jnp.concatenate(
        [
            jnp.stack([grad_shift_first, grad_scale_first, grad_gate_first]).reshape(2, 1536),
            jnp.stack([grad_shift_second, grad_scale_second, grad_gate_second]).reshape(2, 1536),
        ],
        axis=0,
    ).reshape(2, 3072)
    sums = jnp.concatenate(
        [
            sums,
            out_bias_part.reshape(2, 512),
            project_bias_part.reshape(2, 512),
            hidden_bias_part.reshape(2, 1024),
        ],
        axis=1,
    )
    sums = lax.dynamic_index_in_dim(sums, place.c, 0, keepdims=False) + swap_core(
        lax.dynamic_index_in_dim(sums, 1 - place.c, 0, keepdims=False)
    )
    mod_low = sums[:3072].astype(BF16)
    hidden_sum = sums[4096:]
    biases = jnp.concatenate(
        [
            sums[3072:4096],
            jnp.where(on_first, hidden_sum, 0.0),
            jnp.where(on_first, 0.0, hidden_sum),
            attend_bias_part.reshape(1024),
        ]
    ).astype(BF16)
    chunks = jnp.broadcast_to(biases.reshape(32, 1, 128), (32, 2, 128)).reshape(64, 128)
    payload = jnp.concatenate([jnp.broadcast_to(mod_low, (64, 3072)), chunks], axis=1)
    payload = lax.all_to_all(payload, CHIPS, 0, 0, tiled=True)
    bias_chunk = jnp.sum(payload[:, 3072:].astype(F32), axis=0)
    mod_mine = payload[:, :3072]
    mod_theirs = swap_core(mod_mine)
    mod_all = jnp.where(
        place.first,
        jnp.concatenate([mod_mine, mod_theirs], axis=1),
        jnp.concatenate([mod_theirs, mod_mine], axis=1),
    )
    grad_ada = dot_tn(silu_rows, mod_all)[:, None]
    ada_bias_sum = jnp.sum(mod_all.astype(F32), axis=0)[None]
    row_parts = dot_nt(mod_all, modulate)
    payload = jnp.concatenate([row_parts, jnp.broadcast_to(bias_chunk, (64, 128))], axis=1)
    payload = lax.all_to_all(payload, DP, 0, 0, tiled=True)
    grad_silu = payload[:, :16].reshape(1, width)
    _, silu_back = jax.vjp(jax.nn.silu, conditioning.astype(F32))
    grad_conditioning = silu_back(grad_silu)[0].astype(BF16)
    bias_sums = payload[:, 16:].reshape(32, 2, 128).transpose(1, 0, 2).reshape(2, 4096)
    out_bias_sum = bias_sums[:, :512].reshape(1, 1024)
    project_bias_sum = bias_sums[:, 512:1024].reshape(1, 1024)
    hidden_bias_sum = lax.dynamic_index_in_dim(
        bias_sums[:, 1024:3072].reshape(2, 2, 1024), place.t, 1, keepdims=False
    ).reshape(1, 2048)
    attend_bias_sum = lax.dynamic_index_in_dim(
        bias_sums[:, 3072:].reshape(2, 2, 2, 256), place.t, 1, keepdims=False
    )
    attend_bias_sum = attend_bias_sum.transpose(1, 0, 2).reshape(1, 2, 512)

    reduced = scatter_attention(attention_grads, place).reshape(2, 16, 1024)
    mine = lax.dynamic_index_in_dim(reduced, place.c, 0, keepdims=False)
    theirs = swap_core(lax.dynamic_index_in_dim(reduced, 1 - place.c, 0, keepdims=False))
    low = jnp.where(place.first, mine, theirs).reshape(16, 4, 256)
    high = jnp.where(place.first, theirs, mine).reshape(16, 4, 256)
    reduced = jnp.concatenate([low, high], axis=2)

    return (
        block_output,
        grad_latents,
        grad_conditioning,
        grad_ada,
        ada_bias_sum,
        reduced[None, :, :3],
        attend_bias_sum,
        reduced[None, :, 3],
        project_bias_sum,
        forward_grads[0][None],
        hidden_bias_sum,
        forward_grads[1][None],
        out_bias_sum,
    )


def solution(mesh):
    fine = Mesh(mesh.devices.reshape(4, 2, 4, 2, 2), ("z", "w", "y", "c", "t"))
    return jax.shard_map(
        shards,
        mesh=fine,
        in_specs=(
            P(DP, "t", None),
            P(DP, None),
            P(DP, "t", None),
            P(DP, None, None),
            P(),
            P(None, DP, None, "t"),
            P(None, None, "t"),
            P(None, DP, "t"),
            P(),
            P(None, DP, "t"),
            P(None, "t"),
            P(None, DP, "t"),
            P(),
        ),
        out_specs=(
            P(DP, "t", None),
            P(DP, "t", None),
            P(DP, None),
            P(DP, None, None),
            P(),
            P(None, DP, None, "t"),
            P(None, None, "t"),
            P(None, DP, "t"),
            P(),
            P(None, DP, "t"),
            P(None, "t"),
            P(None, DP, "t"),
            P(),
        ),
        check_vma=False,
    )
```

```python
import math

import jax
import jax.numpy as jnp
from jax import lax
from jax.experimental import pallas as pl
from jax.experimental.pallas import tpu as pltpu
from jax.sharding import Mesh
from jax.sharding import PartitionSpec as P

HEAD_DIM = 64
EPS = 1e-06
F32 = jnp.float32
BF16 = jnp.bfloat16
DP = ("z", "w", "y", "c")
CHIPS = ("z", "w", "y", "t")


def normalize(values):
    centered = values - jnp.mean(values, axis=-1, keepdims=True)
    inverse = lax.rsqrt(jnp.mean(centered * centered, axis=-1, keepdims=True) + EPS)
    return (centered * inverse, inverse)


def normalize_back(grad, normed, inverse):
    return inverse * (
        grad
        - jnp.mean(grad, axis=-1, keepdims=True)
        - normed * jnp.mean(grad * normed, axis=-1, keepdims=True)
    )


def dot(left, right):
    return jnp.dot(left, right, preferred_element_type=F32)


def dot_nt(left, right):
    return lax.dot_general(left, right, (((1,), (1,)), ((), ())), preferred_element_type=F32)


def dot_tn(left, right):
    return lax.dot_general(left, right, (((0,), (0,)), ((), ())), preferred_element_type=F32)


def swap_core(piece):
    return lax.ppermute(piece, "c", [(0, 1), (1, 0)])


def swap_t(piece):
    return lax.ppermute(piece, "t", [(0, 1), (1, 0)])


def swap_layout(piece):
    return lax.ppermute(piece, ("c", "t"), [(0, 0), (1, 2), (2, 1), (3, 3)])


def flip_plane(piece, step, last):
    perm = []
    for z in range(4):
        for y in range(4):
            for c in range(2):
                along_z = (c == 0) == last
                z2, y2 = (z ^ step, y) if along_z else (z, y ^ step)
                perm.append(((z * 4 + y) * 2 + c, (z2 * 4 + y2) * 2 + c))
    return lax.ppermute(piece, ("z", "y", "c"), perm)


def flip_x(piece, w_step, t_step):
    perm = [(w * 2 + t, (w ^ w_step) * 2 + (t ^ t_step)) for w in range(2) for t in range(2)]
    return lax.ppermute(piece, ("w", "t"), perm)


STEPS = (2, 1, 3)


def after(values, *others):
    return lax.optimization_barrier((values, others))[0]


def by_step(own, received):
    return [own] + [received[k] for k in (1, 2, 3)]


def one_hot(order):
    features = lax.broadcasted_iota(jnp.int32, (1024, 1024), 0)
    return (features == order[None, :]).astype(BF16)


class Place:
    def __init__(self):
        self.z = lax.axis_index("z")
        self.w = lax.axis_index("w")
        self.y = lax.axis_index("y")
        self.c = lax.axis_index("c")
        self.t = lax.axis_index("t")
        self.first = self.c == 0

    def attention_order(self):
        place = lax.iota(jnp.int32, 1024)
        last, before, w_step, row = place // 256, place // 64 % 4, place // 32 % 2, place % 32
        z = self.z ^ jnp.where(self.first, last, before)
        y = self.y ^ jnp.where(self.first, before, last)
        return ((z * 2 + (self.w ^ w_step)) * 4 + y) * 32 + row

    def forward_order(self):
        place = lax.iota(jnp.int32, 1024)
        core = self.c ^ (place // 512)
        last, before, w_step, row = place // 128 % 4, place // 32 % 4, place // 16 % 2, place % 16
        z = self.z ^ jnp.where(core == 0, last, before)
        y = self.y ^ jnp.where(core == 0, before, last)
        return ((z * 2 + (self.w ^ w_step)) * 4 + y) * 32 + core * 16 + row


def add_up(own, received):
    total = own.astype(F32)
    for block in received:
        total = total + block.astype(F32)
    return total


def send_plane(blocks, last):
    return {k: flip_plane(blocks[k], k, last) for k in STEPS}


def reduce_plane(blocks, last):
    return add_up(blocks[0], send_plane(blocks, last).values())


TOKENS = 256
WIDTH = 1024
BLOCK = 256
ALL_HEADS = [(t, h) for t in range(2) for h in range(4)]
SCALE = HEAD_DIM ** (-0.5)


def head_columns(t, h):
    return slice(t * 256 + h * HEAD_DIM, t * 256 + (h + 1) * HEAD_DIM)


def forward_kernel(first, order, w0, w1, w2, w3, bias, rel, query, key, value, probs, mixed, out):
    blocks = (w0, w1, w2, w3)
    rel[...] = dot(first[...], order[...]).astype(BF16)
    for t in range(2):
        packed = sum(
            dot(rel[:, k * BLOCK : (k + 1) * BLOCK], blocks[k][t, :, :768]) for k in range(4)
        )
        columns = slice(t * 256, (t + 1) * 256)
        query[:, columns] = (packed[:, :256] + bias[0:1, columns]).astype(BF16)
        key[:, columns] = packed[:, 256:512].astype(BF16)
        value[:, columns] = (packed[:, 512:768] + bias[1:2, columns]).astype(BF16)
    for t, h in ALL_HEADS:
        columns = head_columns(t, h)
        scores = dot_nt(query[:, columns], key[:, columns]) * SCALE
        expd = jnp.exp(scores - jnp.max(scores, axis=-1, keepdims=True))
        prob = expd / jnp.sum(expd, axis=-1, keepdims=True)
        probs[t * 4 + h] = prob
        mixed[:, columns] = dot(prob.astype(BF16), value[:, columns]).astype(BF16)
    partial = [
        sum(
            dot_nt(mixed[:, t * 256 : (t + 1) * 256], blocks[k][t, :, 768:]) for t in range(2)
        ).astype(BF16)
        for k in range(4)
    ]
    out[...] = dot_nt(jnp.concatenate(partial, axis=1), order[...]).astype(BF16)


def backward_kernel(
    projected, order, w0, w1, w2, w3, rel, query, key, value, probs, mixed,
    g0, g1, g2, g3, out, bias, packed, back,
):
    blocks = (w0, w1, w2, w3)
    grads = (g0, g1, g2, g3)
    back[...] = dot(projected[...], order[...]).astype(BF16)
    for t in range(2):
        grad_mixed = sum(
            dot(back[:, k * BLOCK : (k + 1) * BLOCK], blocks[k][t, :, 768:]) for k in range(4)
        ).astype(BF16)
        for h in range(4):
            columns = head_columns(t, h)
            grad_head = grad_mixed[:, h * HEAD_DIM : (h + 1) * HEAD_DIM]
            prob = probs[t * 4 + h]
            grad_value = dot_tn(prob.astype(BF16), grad_head)
            grad_probs = dot_nt(grad_head, value[:, columns])
            grad_scores = (
                prob * (grad_probs - jnp.sum(grad_probs * prob, axis=-1, keepdims=True))
            ).astype(BF16)
            grad_query = dot(grad_scores, key[:, columns]) * SCALE
            grad_key = dot_tn(grad_scores, query[:, columns]) * SCALE
            for i, item in enumerate((grad_query, grad_key, grad_value)):
                begin = i * 256 + h * HEAD_DIM
                packed[t, :, begin : begin + HEAD_DIM] = item.astype(BF16)
        for row, begin in enumerate((0, 512)):
            bias[t * 2 + row : t * 2 + row + 1, :] = jnp.sum(
                packed[t, :, begin : begin + 256].astype(F32), axis=0, keepdims=True
            )
    partial = []
    for k in range(4):
        rows = slice(k * BLOCK, (k + 1) * BLOCK)
        for t in range(2):
            grads[k][:, t * 1024 : t * 1024 + 768] = dot_tn(rel[:, rows], packed[t]).astype(BF16)
            grads[k][:, t * 1024 + 768 : (t + 1) * 1024] = dot_tn(
                back[:, rows], mixed[:, t * 256 : (t + 1) * 256]
            ).astype(BF16)
        partial.append(
            sum(dot_nt(packed[t], blocks[k][t, :, :768]) for t in range(2)).astype(BF16)
        )
    out[...] = dot_nt(jnp.concatenate(partial, axis=1), order[...]).astype(BF16)


def middle_kernel(
    second, branch, order, hidden, m0, m1, m2, m3, t0, t1, t2, t3,
    rel, active, grad_pre, out, back, hidden_sum, mine, theirs, arrived,
):
    copies = []
    for which in range(2):
        for half, (target, blocks) in enumerate(((mine, (m0, m1, m2, m3)), (theirs, (t0, t1, t2, t3)))):
            for k, block in enumerate(blocks):
                copies.append(
                    pltpu.make_async_copy(
                        block.at[which],
                        target.at[which, pl.ds(k * 128, 128)],
                        arrived.at[which * 8 + half * 4 + k],
                    )
                )
    for copy in copies:
        copy.start()
    rel[...] = dot(second[...], order[...]).astype(BF16)
    for copy in copies:
        copy.wait()
    root = (2.0 / math.pi) ** 0.5
    for begin in range(0, 2048, 512):
        columns = slice(begin, begin + 512)
        pre = (
            dot(rel[:, :512], mine[0, :, columns])
            + dot(rel[:, 512:], theirs[0, :, columns])
            + hidden[0:1, columns]
        )
        grad_active = dot(branch[:, :512], mine[1, :, columns]) + dot(
            branch[:, 512:], theirs[1, :, columns]
        )
        square = pre * pre
        bent = jnp.tanh(root * (pre + 0.044715 * (square * pre)))
        half = 0.5 * (1.0 + bent)
        active[:, columns] = (pre * half).astype(BF16)
        slope = half + (0.5 * pre) * (1.0 - bent * bent) * (root * (1.0 + 0.134145 * square))
        low = (grad_active * slope).astype(BF16)
        grad_pre[:, columns] = low
        hidden_sum[0:1, columns] = jnp.sum(low.astype(F32), axis=0, keepdims=True)
    for source, which, target in ((grad_pre, 0, back), (active, 1, out)):
        partial = jnp.concatenate(
            [dot_nt(source[...], item[which]).astype(BF16) for item in (mine, theirs)], axis=1
        )
        target[...] = dot_nt(partial, order[...]).astype(BF16)


def shaped(shape, kind=BF16):
    return jax.ShapeDtypeStruct(shape, kind)


def call(kernel, outs, args, flops, scratch=(), near=100):
    whole = pl.BlockSpec(memory_space=pltpu.VMEM)
    moved = sum(item.size * item.dtype.itemsize for item in (*args, *outs))
    return pl.pallas_call(
        kernel,
        out_shape=outs,
        in_specs=[whole if i < near else pl.BlockSpec(memory_space=pl.ANY) for i in range(len(args))],
        out_specs=[whole] * len(outs),
        scratch_shapes=list(scratch),
        compiler_params=pltpu.CompilerParams(vmem_limit_bytes=28 * 2**20),
        cost_estimate=pl.CostEstimate(flops=flops, bytes_accessed=moved, transcendentals=0),
    )(*args)


def attention_forward(first, order, blocks, bias):
    half = shaped((TOKENS, 512))
    outs = (
        shaped((TOKENS, WIDTH)), half, half, half, shaped((8, TOKENS, TOKENS), F32), half,
        shaped((TOKENS, WIDTH)),
    )
    return call(forward_kernel, outs, (first, order, *blocks, bias), 4 * 10**9)


def attention_backward(projected, order, blocks, saved):
    outs = (shaped((BLOCK, 2048)),) * 4 + (shaped((TOKENS, WIDTH)), shaped((4, 256), F32))
    scratch = (pltpu.VMEM((2, TOKENS, 768), BF16), pltpu.VMEM((TOKENS, WIDTH), BF16))
    return call(backward_kernel, outs, (projected, order, *blocks, *saved), 4 * 10**9, scratch)


def feed_forward(second, branch, order, hidden, mine, theirs):
    wide, narrow = shaped((TOKENS, 2048)), shaped((TOKENS, WIDTH))
    outs = (narrow, wide, wide, narrow, narrow, shaped((1, 2048), F32))
    scratch = (
        pltpu.VMEM((2, 512, 2048), BF16),
        pltpu.VMEM((2, 512, 2048), BF16),
        pltpu.SemaphoreType.DMA((16,)),
    )
    args = (second, branch, order, hidden, *mine, *theirs)
    return call(middle_kernel, outs, args, 6 * 10**9, scratch, 4)


def halves(rows):
    half = rows.shape[0] // 2
    return rows[:half], rows[half:]


def shards(
    latents,
    conditioning,
    cotangent,
    modulate_weight,
    modulate_bias,
    attend_weight,
    attend_bias,
    project_weight,
    project_bias,
    hidden_weight,
    hidden_bias,
    output_weight,
    output_bias,
):
    place = Place()
    width = conditioning.shape[1]

    modulate = modulate_weight[:, 0]
    order_a = one_hot(place.attention_order())
    order_f = one_hot(place.forward_order())

    quarters = jnp.concatenate(
        [attend_weight[0].reshape(16, 3, 2, 256), project_weight[0].reshape(16, 1, 2, 256)], axis=1
    )
    mine = lax.dynamic_index_in_dim(quarters, place.c, 2, keepdims=False).reshape(16, 1024)
    theirs = lax.dynamic_index_in_dim(quarters, 1 - place.c, 2, keepdims=False).reshape(16, 1024)
    theirs = swap_core(theirs)
    piece = jnp.where(
        place.first, jnp.concatenate([mine, theirs]), jnp.concatenate([theirs, mine])
    )
    flipped_t, flipped_w, flipped_both = (
        flip_x(piece, 0, 1),
        flip_x(piece, 1, 0),
        flip_x(piece, 1, 1),
    )
    attend_one = jnp.stack(
        [jnp.stack([piece, flipped_w]), jnp.stack([flipped_t, flipped_both])]
    )[:, None]
    forward_piece = jnp.stack([hidden_weight[0], output_weight[0]])
    forward_one = jnp.stack([forward_piece, flip_x(forward_piece, 1, 0)], axis=1)[:, None]

    silu_rows = lax.all_to_all(after(conditioning, attend_one, forward_one).reshape(64, 16), DP, 0, 0, tiled=True)
    silu_rows = jax.nn.silu(silu_rows.astype(F32)).astype(BF16)

    attend_two = jnp.concatenate(
        by_step(attend_one, {k: flip_plane(attend_one, k, False) for k in STEPS}), axis=1
    )
    forward_two = jnp.concatenate(
        by_step(forward_one, {k: flip_plane(forward_one, k, False) for k in STEPS}), axis=1
    )
    attend_two = after(attend_two, silu_rows, forward_two)
    attend_blocks = by_step(attend_two, {k: flip_plane(attend_two, k, True) for k in STEPS})
    attend_blocks = [item.reshape(2, BLOCK, WIDTH) for item in attend_blocks]

    silu_chip = lax.dynamic_index_in_dim(silu_rows.reshape(32, 2, 16), place.t, 1, keepdims=False)
    terms = dot(silu_chip, modulate).reshape(64, 24, 128)
    terms = lax.all_to_all(after(terms, attend_two), DP, 0, 0)
    mods_half = jnp.sum(terms, axis=0).reshape(3072)
    mods = lax.all_gather(mods_half, "c", axis=0, tiled=True) + modulate_bias[0].astype(F32)
    mods = mods.reshape(6, width)

    bias_own = lax.dynamic_slice_in_dim(attend_bias[0], place.c * 256, 256, 1)
    bias_pair = jnp.concatenate([bias_own, swap_t(bias_own)], axis=1).astype(F32)
    on_first = place.t == 0

    stream = swap_layout(latents[0]).astype(F32)
    grad = swap_layout(cotangent[0]).astype(F32)

    normed_first, inverse_first = normalize(stream)
    first_in = (normed_first * (1.0 + mods[1]) + mods[0]).astype(BF16)
    first_all = jnp.concatenate([first_in, swap_core(first_in)])
    forward_two = after(forward_two, attend_blocks, first_all)
    forward_got = {k: flip_plane(forward_two, k, True) for k in STEPS}
    grad_branch = (grad * mods[5]).astype(BF16)
    out_bias_part = jnp.sum(grad_branch.astype(F32), axis=0)
    branch_all = jnp.concatenate([grad_branch, swap_t(grad_branch)])
    branch_rel = dot(branch_all, order_f).astype(BF16)
    first_rel, query, key, value, probs, mixed, partial = attention_forward(
        first_all, order_a, attend_blocks, bias_pair
    )
    own, other = halves(partial)
    projected = own.astype(F32) + swap_core(other).astype(F32) + project_bias[0].astype(F32)
    middle = stream + mods[2] * projected

    normed_second, inverse_second = normalize(middle)
    second_in = (normed_second * (1.0 + mods[4]) + mods[3]).astype(BF16)
    second_in = after(second_in, branch_rel)
    forward_got = after(forward_got, second_in)
    forward_mine = [item.reshape(2, 128, 2048) for item in by_step(forward_two, forward_got)]
    forward_theirs = [swap_core(item) for item in forward_mine]
    second_all = jnp.concatenate([second_in, swap_t(second_in)])
    second_rel, active, grad_pre, branch_partial, back_partial, hidden_bias_part = feed_forward(
        second_all, branch_rel, order_f, hidden_bias.astype(F32), forward_mine, forward_theirs
    )
    def core_sum(rows, columns):
        theirs = swap_core(dot_tn(rows[:, 512:], columns).astype(BF16))
        mine = (dot_tn(rows[:, :512], columns) + theirs.astype(F32)).astype(BF16)
        return [mine[k * 128 : (k + 1) * 128] for k in range(4)]

    down_blocks = core_sum(branch_rel, active)
    down_got = send_plane(down_blocks, True)
    up_blocks = core_sum(second_rel, grad_pre)
    up_got = send_plane(up_blocks, True)
    own, other = halves(back_partial)
    received = after(swap_t(other), down_blocks, up_blocks)
    grad_second = own.astype(F32) + received.astype(F32)
    grad_shift_second = jnp.sum(grad_second, axis=0)
    grad_scale_second = jnp.sum(grad_second * normed_second, axis=0)
    grad_middle = grad + normalize_back(
        grad_second * (1.0 + mods[4]), normed_second, inverse_second
    )

    grad_gate_first = jnp.sum(grad_middle * projected, axis=0)
    grad_projected = (grad_middle * mods[2]).astype(BF16)
    project_bias_part = jnp.sum(grad_projected.astype(F32), axis=0)
    projected_all = jnp.concatenate([grad_projected, swap_core(grad_projected)])
    *attend_grads, partial, attend_bias_part = attention_backward(
        projected_all,
        order_a,
        attend_blocks,
        (first_rel, query, key, value, probs, mixed),
    )
    attend_grads = after(attend_grads, up_got, down_got)
    attend_got = send_plane(attend_grads, True)
    branch_own, other = halves(branch_partial)
    other = after(other, grad_projected)
    received = after(swap_t(other), partial)
    branch = branch_own.astype(F32) + received.astype(F32) + output_bias[0].astype(F32)
    block_output = swap_layout((middle + mods[5] * branch).astype(BF16))[None]
    grad_gate_second = jnp.sum(grad * branch, axis=0)
    own, other = halves(partial)
    grad_first = own.astype(F32) + swap_core(other).astype(F32)
    attend_bias_part = attend_bias_part.reshape(2, 2, 256)
    attend_bias_part = jnp.where(on_first, attend_bias_part, attend_bias_part[::-1])
    grad_shift_first = jnp.sum(grad_first, axis=0)
    grad_scale_first = jnp.sum(grad_first * normed_first, axis=0)
    grad_stream = grad_middle + normalize_back(
        grad_first * (1.0 + mods[1]), normed_first, inverse_first
    )
    grad_latents = swap_layout(grad_stream.astype(BF16))[None]

    sums = jnp.concatenate(
        [
            jnp.stack([grad_shift_first, grad_scale_first, grad_gate_first]).reshape(2, 1536),
            jnp.stack([grad_shift_second, grad_scale_second, grad_gate_second]).reshape(2, 1536),
        ],
        axis=0,
    ).reshape(2, 3072)
    sums = jnp.concatenate(
        [
            sums,
            out_bias_part.reshape(2, 512),
            project_bias_part.reshape(2, 512),
            hidden_bias_part.reshape(2, 1024),
        ],
        axis=1,
    )
    sums = lax.dynamic_index_in_dim(sums, place.c, 0, keepdims=False) + swap_core(
        lax.dynamic_index_in_dim(sums, 1 - place.c, 0, keepdims=False)
    )
    mod_low = sums[:3072].astype(BF16)
    hidden_sum = sums[4096:]
    biases = jnp.concatenate(
        [
            sums[3072:4096],
            jnp.where(on_first, hidden_sum, 0.0),
            jnp.where(on_first, 0.0, hidden_sum),
            attend_bias_part.reshape(1024),
        ]
    ).astype(BF16)
    chunks = jnp.broadcast_to(biases.reshape(32, 1, 128), (32, 2, 128)).reshape(64, 128)
    payload = jnp.concatenate(
        [jnp.broadcast_to(mod_low.reshape(24, 128), (64, 24, 128)), chunks[:, None]], axis=1
    )
    payload, attend_got = lax.optimization_barrier((payload, attend_got))
    up_got, down_got = after((up_got, down_got), payload)
    forward_sum = jnp.stack(
        [
            add_up(up_blocks[0], up_got.values()),
            add_up(down_blocks[0], down_got.values()),
        ]
    ).astype(BF16)
    forward_sum = reduce_plane([forward_sum[:, k * 32 : (k + 1) * 32] for k in range(4)], False)
    forward_grads = forward_sum[:, :16] + flip_x(forward_sum[:, 16:].astype(BF16), 1, 0).astype(F32)

    payload = lax.all_to_all(payload, CHIPS, 0, 0)

    attend_sum = add_up(attend_grads[0], attend_got.values()).astype(BF16)
    attend_two = reduce_plane([attend_sum[k * 64 : (k + 1) * 64] for k in range(4)], False)

    def pick(w_step, t_step):
        return attend_two[w_step * 32 : (w_step + 1) * 32, t_step * 1024 : (t_step + 1) * 1024]

    reduced = add_up(
        pick(0, 0),
        [flip_x(pick(w, t).astype(BF16), w, t) for w, t in ((0, 1), (1, 0), (1, 1))],
    ).reshape(2, 16, 1024)
    mine = lax.dynamic_index_in_dim(reduced, place.c, 0, keepdims=False)
    theirs = swap_core(lax.dynamic_index_in_dim(reduced, 1 - place.c, 0, keepdims=False))
    low = jnp.where(place.first, mine, theirs).reshape(16, 4, 256)
    high = jnp.where(place.first, theirs, mine).reshape(16, 4, 256)
    reduced = jnp.concatenate([low, high], axis=2)


    bias_chunk = jnp.sum(payload[:, 24].astype(F32), axis=0)
    mod_mine = payload[:, :24].reshape(64, 3072)
    mod_theirs = swap_core(mod_mine)
    mod_all = jnp.where(
        place.first,
        jnp.concatenate([mod_mine, mod_theirs], axis=1),
        jnp.concatenate([mod_theirs, mod_mine], axis=1),
    )
    grad_ada = dot_tn(silu_rows, mod_all)[:, None]
    ada_bias_sum = jnp.sum(mod_all.astype(F32), axis=0)[None]
    row_parts = dot_nt(mod_all, modulate)
    payload = jnp.stack(
        [jnp.pad(row_parts, ((0, 0), (0, 112))), jnp.broadcast_to(bias_chunk, (64, 128))], axis=1
    )
    payload = lax.all_to_all(payload, DP, 0, 0)
    grad_silu = payload[:, 0, :16].reshape(1, width)
    _, silu_back = jax.vjp(jax.nn.silu, conditioning.astype(F32))
    grad_conditioning = silu_back(grad_silu)[0].astype(BF16)
    bias_sums = payload[:, 1].reshape(32, 2, 128).transpose(1, 0, 2).reshape(2, 4096)
    out_bias_sum = bias_sums[:, :512].reshape(1, 1024)
    project_bias_sum = bias_sums[:, 512:1024].reshape(1, 1024)
    hidden_bias_sum = lax.dynamic_index_in_dim(
        bias_sums[:, 1024:3072].reshape(2, 2, 1024), place.t, 1, keepdims=False
    ).reshape(1, 2048)
    attend_bias_sum = lax.dynamic_index_in_dim(
        bias_sums[:, 3072:].reshape(2, 2, 2, 256), place.t, 1, keepdims=False
    )
    attend_bias_sum = attend_bias_sum.transpose(1, 0, 2).reshape(1, 2, 512)

    return (
        block_output,
        grad_latents,
        grad_conditioning,
        grad_ada,
        ada_bias_sum,
        reduced[None, :, :3],
        attend_bias_sum,
        reduced[None, :, 3],
        project_bias_sum,
        forward_grads[0][None],
        hidden_bias_sum,
        forward_grads[1][None],
        out_bias_sum,
    )


def solution(mesh):
    fine = Mesh(mesh.devices.reshape(4, 2, 4, 2, 2), ("z", "w", "y", "c", "t"))
    return jax.shard_map(
        shards,
        mesh=fine,
        in_specs=(
            P(DP, "t", None),
            P(DP, None),
            P(DP, "t", None),
            P(DP, None, None),
            P(),
            P(None, DP, None, "t"),
            P(None, None, "t"),
            P(None, DP, "t"),
            P(),
            P(None, DP, "t"),
            P(None, "t"),
            P(None, DP, "t"),
            P(),
        ),
        out_specs=(
            P(DP, "t", None),
            P(DP, "t", None),
            P(DP, None),
            P(DP, None, None),
            P(),
            P(None, DP, None, "t"),
            P(None, None, "t"),
            P(None, DP, "t"),
            P(),
            P(None, DP, "t"),
            P(None, "t"),
            P(None, DP, "t"),
            P(),
        ),
        check_vma=False,
    )
```

```python
import functools
import math

import jax
import jax.numpy as jnp
from jax import lax
from jax.experimental import pallas as pl
from jax.experimental.pallas import tpu as pltpu
from jax.sharding import Mesh
from jax.sharding import PartitionSpec as P

HEAD_DIM = 64
EPS = 1e-06
F32 = jnp.float32
BF16 = jnp.bfloat16
DP = ("z", "w", "y", "c")
CHIPS = ("z", "w", "y", "t")


def normalize(values):
    centered = values - jnp.mean(values, axis=-1, keepdims=True)
    inverse = lax.rsqrt(jnp.mean(centered * centered, axis=-1, keepdims=True) + EPS)
    return (centered * inverse, inverse)


def normalize_back(grad, normed, inverse):
    return inverse * (
        grad
        - jnp.mean(grad, axis=-1, keepdims=True)
        - normed * jnp.mean(grad * normed, axis=-1, keepdims=True)
    )


def dot(left, right):
    return jnp.dot(left, right, preferred_element_type=F32)


def dot_nt(left, right):
    return lax.dot_general(left, right, (((1,), (1,)), ((), ())), preferred_element_type=F32)


def dot_tn(left, right):
    return lax.dot_general(left, right, (((0,), (0,)), ((), ())), preferred_element_type=F32)


def swap_core(piece):
    return lax.ppermute(piece, "c", [(0, 1), (1, 0)])


def swap_t(piece):
    return lax.ppermute(piece, "t", [(0, 1), (1, 0)])


def swap_layout(piece):
    return lax.ppermute(piece, ("c", "t"), [(0, 0), (1, 2), (2, 1), (3, 3)])


def flip_plane(piece, step, last):
    perm = []
    for z in range(4):
        for y in range(4):
            for c in range(2):
                along_z = (c == 0) == last
                z2, y2 = (z ^ step, y) if along_z else (z, y ^ step)
                perm.append(((z * 4 + y) * 2 + c, (z2 * 4 + y2) * 2 + c))
    return lax.ppermute(piece, ("z", "y", "c"), perm)


def flip_x(piece, w_step, t_step):
    perm = [(w * 2 + t, (w ^ w_step) * 2 + (t ^ t_step)) for w in range(2) for t in range(2)]
    return lax.ppermute(piece, ("w", "t"), perm)


STEPS = (2, 1, 3)


def after(value, *others):
    def copy(source, *rest):
        rest[-1][...] = source[...]

    whole = pl.BlockSpec(memory_space=pltpu.VMEM)
    left = pl.BlockSpec(memory_space=pl.ANY)
    return pl.pallas_call(
        copy,
        out_shape=jax.ShapeDtypeStruct(value.shape, value.dtype),
        in_specs=[whole] + [left] * len(others),
        out_specs=whole,
    )(value, *others)


def by_step(own, received):
    return [own] + [received[k] for k in (1, 2, 3)]


def one_hot(order):
    features = lax.broadcasted_iota(jnp.int32, (1024, 1024), 0)
    return (features == order[None, :]).astype(BF16)


class Place:
    def __init__(self):
        self.z = lax.axis_index("z")
        self.w = lax.axis_index("w")
        self.y = lax.axis_index("y")
        self.c = lax.axis_index("c")
        self.t = lax.axis_index("t")
        self.first = self.c == 0

    def attention_order(self):
        place = lax.iota(jnp.int32, 1024)
        last, before, w_step, row = place // 256, place // 64 % 4, place // 32 % 2, place % 32
        z = self.z ^ jnp.where(self.first, last, before)
        y = self.y ^ jnp.where(self.first, before, last)
        return ((z * 2 + (self.w ^ w_step)) * 4 + y) * 32 + row

    def forward_order(self):
        place = lax.iota(jnp.int32, 1024)
        core = self.c ^ (place // 512)
        last, before, w_step, row = place // 128 % 4, place // 32 % 4, place // 16 % 2, place % 16
        z = self.z ^ jnp.where(core == 0, last, before)
        y = self.y ^ jnp.where(core == 0, before, last)
        return ((z * 2 + (self.w ^ w_step)) * 4 + y) * 32 + core * 16 + row


def add_up(own, received):
    total = own.astype(F32)
    for block in received:
        total = total + block.astype(F32)
    return total


def send_plane(blocks, last):
    return {k: flip_plane(blocks[k], k, last) for k in STEPS}


def reduce_plane(blocks, last):
    return add_up(blocks[0], send_plane(blocks, last).values())


TOKENS = 256
WIDTH = 1024
BLOCK = 256
ALL_HEADS = [(t, h) for t in range(2) for h in range(4)]
SCALE = HEAD_DIM ** (-0.5)


def head_columns(t, h):
    return slice(t * 256 + h * HEAD_DIM, t * 256 + (h + 1) * HEAD_DIM)


def weight_rows(block, t, columns):
    rows = [block[k // 2, (k % 2) * 128 + t * 64 : (k % 2) * 128 + (t + 1) * 64, columns] for k in range(4)]
    return jnp.concatenate(rows)


TRIPLE, PROJECT = slice(0, 768), slice(768, 1024)


def places(kept, kept_probs):
    left, right = pl.ds(0, 512), pl.ds(512, 512)
    return (
        kept.at[0],
        kept.at[1, :, left],
        kept.at[1, :, right],
        kept.at[2, :, left],
        kept_probs.at[pl.ds(0, 8)],
        kept.at[2, :, right],
        *(kept.at[pl.ds(4 + 2 * k, 2)] for k in range(4)),
    )


def forward_kernel(
    first, order, w0, w1, w2, w3, bias, one,
    kept, kept_probs, out, rel, query, key, value, probs, mixed, sent,
):
    blocks = (w0, w1, w2, w3)
    copies = [
        pltpu.make_async_copy(source, target, sent.at[i])
        for i, (source, target) in enumerate(
            zip((rel, query, key, value, probs, mixed, *blocks), places(kept, kept_probs))
        )
    ]
    for copy in copies[6:]:
        copy.start()
    rel[...] = dot(first[...], order[...]).astype(BF16)
    copies[0].start()
    for t in range(2):
        packed = sum(
            dot(rel[:, k * BLOCK : (k + 1) * BLOCK], weight_rows(blocks[k], t, TRIPLE))
            for k in range(4)
        )
        columns = slice(t * 256, (t + 1) * 256)
        query[:, columns] = (packed[:, :256] + bias[0:1, columns]).astype(BF16)
        key[:, columns] = packed[:, 256:512].astype(BF16)
        value[:, columns] = (packed[:, 512:768] + bias[1:2, columns]).astype(BF16)
    for copy in copies[1:4]:
        copy.start()
    for t, h in ALL_HEADS:
        columns = head_columns(t, h)
        scores = dot_nt(query[:, columns], key[:, columns]) * SCALE
        expd = jnp.exp(scores - jnp.max(scores, axis=-1, keepdims=True))
        prob = expd / jnp.sum(expd, axis=-1, keepdims=True)
        probs[t * 4 + h] = prob
        mixed[:, columns] = dot(prob.astype(BF16), value[:, columns]).astype(BF16)
    for copy in copies[4:6]:
        copy.start()
    partial = [
        sum(
            dot_nt(mixed[:, t * 256 : (t + 1) * 256], weight_rows(blocks[k], t, PROJECT))
            for t in range(2)
        ).astype(BF16)
        for k in range(4)
    ]
    out[...] = dot_nt(jnp.concatenate(partial, axis=1), order[...]).astype(BF16)
    for copy in copies:
        copy.wait()


def backward_kernel(
    projected, order, kept, kept_probs, one, g0, g1, g2, g3, out, bias,
    packed, back, ready, w0, w1, w2, w3, rel, query, key, value, probs, mixed, sent, arrived,
):
    blocks = (w0, w1, w2, w3)
    fetched = [
        pltpu.make_async_copy(source, target, arrived.at[i])
        for i, (source, target) in enumerate(
            zip(
                places(kept, kept_probs),
                (rel, query, key, value, probs, mixed, w0, w1, w2, w3),
            )
        )
    ]
    for copy in fetched:
        copy.start()
    copies = [
        pltpu.make_async_copy(ready.at[k], target, sent.at[k])
        for k, target in enumerate((g0, g1, g2, g3))
    ]
    back[...] = dot(projected[...], order[...]).astype(BF16)
    for copy in fetched:
        copy.wait()
    for t in range(2):
        grad_mixed = sum(
            dot(back[:, k * BLOCK : (k + 1) * BLOCK], weight_rows(blocks[k], t, PROJECT))
            for k in range(4)
        ).astype(BF16)
        for h in range(4):
            columns = head_columns(t, h)
            grad_head = grad_mixed[:, h * HEAD_DIM : (h + 1) * HEAD_DIM]
            prob = probs[t * 4 + h]
            grad_value = dot_tn(prob.astype(BF16), grad_head)
            grad_probs = dot_nt(grad_head, value[:, columns])
            grad_scores = (
                prob * (grad_probs - jnp.sum(grad_probs * prob, axis=-1, keepdims=True))
            ).astype(BF16)
            grad_query = dot(grad_scores, key[:, columns]) * SCALE
            grad_key = dot_tn(grad_scores, query[:, columns]) * SCALE
            for i, item in enumerate((grad_query, grad_key, grad_value)):
                begin = i * 256 + h * HEAD_DIM
                packed[t, :, begin : begin + HEAD_DIM] = item.astype(BF16)
        for row, begin in enumerate((0, 512)):
            bias[t * 2 + row : t * 2 + row + 1, :] = jnp.sum(
                packed[t, :, begin : begin + 256].astype(F32), axis=0, keepdims=True
            )
    partial = []
    for k in range(4):
        rows = slice(k * BLOCK, (k + 1) * BLOCK)
        for t in range(2):
            ready[k, :, t * 1024 : t * 1024 + 768] = dot_tn(rel[:, rows], packed[t]).astype(BF16)
            ready[k, :, t * 1024 + 768 : (t + 1) * 1024] = dot_tn(
                back[:, rows], mixed[:, t * 256 : (t + 1) * 256]
            ).astype(BF16)
        copies[k].start()
        partial.append(
            sum(dot_nt(packed[t], weight_rows(blocks[k], t, TRIPLE)) for t in range(2)).astype(BF16)
        )
    out[...] = dot_nt(jnp.concatenate(partial, axis=1), order[...]).astype(BF16)
    for copy in copies:
        copy.wait()


def middle_kernel(
    second, branch, order, hidden, m0, m1, m2, m3, t0, t1, t2, t3,
    rel, active, out, back, hidden_sum, mine, theirs, arrived,
):
    copies = []
    for which in range(2):
        for half in range(2):
            for target, blocks in ((mine, (m0, m1, m2, m3)), (theirs, (t0, t1, t2, t3))):
                for k, block in enumerate(blocks):
                    copies.append(
                        pltpu.make_async_copy(
                            block.at[:, :, which * 2 + half],
                            target.at[which, k, :, :, :, pl.ds(half * 1024, 1024)],
                            arrived.at[len(copies)],
                        )
                    )
    for copy in copies:
        copy.start()
    rel[0] = dot(second[...], order[...]).astype(BF16)
    rel[1] = dot(branch[...], order[...]).astype(BF16)
    for copy in copies:
        copy.wait()

    def rows(source, which, columns):
        return source[which, :, :, :, :, columns].reshape(512, columns.stop - columns.start)

    root = (2.0 / math.pi) ** 0.5
    for begin in range(0, 2048, 512):
        columns = slice(begin, begin + 512)
        pre = (
            dot(rel[0, :, :512], rows(mine, 0, columns))
            + dot(rel[0, :, 512:], rows(theirs, 0, columns))
            + hidden[0:1, columns]
        )
        grad_active = dot(rel[1, :, :512], rows(mine, 1, columns)) + dot(
            rel[1, :, 512:], rows(theirs, 1, columns)
        )
        square = pre * pre
        bent = jnp.tanh(root * (pre + 0.044715 * (square * pre)))
        half = 0.5 * (1.0 + bent)
        active[1, :, columns] = (pre * half).astype(BF16)
        slope = half + (0.5 * pre) * (1.0 - bent * bent) * (root * (1.0 + 0.134145 * square))
        low = (grad_active * slope).astype(BF16)
        active[0, :, columns] = low
        hidden_sum[0:1, columns] = jnp.sum(low.astype(F32), axis=0, keepdims=True)
    for which, target in ((0, back), (1, out)):
        partial = jnp.concatenate(
            [
                dot_nt(active[which], rows(item, which, slice(0, 2048))).astype(BF16)
                for item in (mine, theirs)
            ],
            axis=1,
        )
        target[...] = dot_nt(partial, order[...]).astype(BF16)


def rows_kernel(rel, columns, theirs, *outs):
    for k, out in enumerate(outs):
        rows = slice(k * 128, (k + 1) * 128)
        for which in range(2):
            out[which] = (
                dot_tn(rel[which, :, rows], columns[which]) + theirs[which, rows].astype(F32)
            ).astype(BF16)


def total_of(blocks, *index):
    return sum(block[index].astype(F32) for block in blocks)


def join_sums_kernel(*refs):
    attend, forward, outs = refs[:4], refs[4:8], refs[-4:]
    for k, out in enumerate(outs):
        out[0:64] = total_of(attend, slice(k * 64, (k + 1) * 64)).astype(BF16)
        for which in range(2):
            rows = slice(k * 32, (k + 1) * 32)
            out[64 + which * 32 : 96 + which * 32] = total_of(forward, which, rows).astype(BF16)


def last_sums_kernel(b0, b1, b2, b3, one, attend_own, forward_own, for_t, for_w, for_both):
    blocks = (b0, b1, b2, b3)
    low, high = slice(0, 1024), slice(1024, 2048)
    attend_own[...] = total_of(blocks, slice(0, 32), low)
    for_t[...] = total_of(blocks, slice(0, 32), high).astype(BF16)
    for_w[0:32] = total_of(blocks, slice(32, 64), low).astype(BF16)
    for_both[...] = total_of(blocks, slice(32, 64), high).astype(BF16)
    for which in range(2):
        begin = 64 + which * 32
        forward_own[which] = total_of(blocks, slice(begin, begin + 16))
        for half, columns in enumerate((low, high)):
            at = 32 + (which * 2 + half) * 16
            for_w[at : at + 16] = total_of(blocks, slice(begin + 16, begin + 32), columns).astype(
                BF16
            )


def split_kernel(core, attend, project, hidden, output, mine, theirs, forward):
    first = core[0] == 0
    for j in range(4):
        rows = attend[:, j, :] if j < 3 else project[...]
        low, high = rows[:, :256], rows[:, 256:]
        mine[:, j * 256 : (j + 1) * 256] = jnp.where(first, low, high)
        theirs[:, j * 256 : (j + 1) * 256] = jnp.where(first, high, low)
    for which, source in enumerate((hidden, output)):
        for half in range(2):
            begin = (which * 2 + half) * 16
            forward[begin : begin + 16] = source[:, half * 1024 : (half + 1) * 1024]


def join_kernel(core, mine, theirs, forward, bias, piece, for_t, for_w):
    first = core[0] == 0
    for target in (piece, for_t, for_w):
        target[0:16] = jnp.where(first, mine[...], theirs[...])
        target[16:32] = jnp.where(first, theirs[...], mine[...])
    for_t[32:48] = bias[...]
    for_w[32:96] = forward[...]


def pack_kernel(plan, *refs):
    outs = refs[len(refs) - len(plan) :]
    for out, parts in zip(outs, plan):
        at = 0
        for source, begin, rows in parts:
            out[at : at + rows] = refs[source][begin : begin + rows]
            at += rows


def shaped(shape, kind=BF16):
    return jax.ShapeDtypeStruct(shape, kind)


def call(kernel, outs, args, flops, scratch=(), far=(), out_far=0, core=(), limit=12):
    whole = pl.BlockSpec(memory_space=pltpu.VMEM)
    left = pl.BlockSpec(memory_space=pl.ANY)
    moved = sum(item.size * item.dtype.itemsize for item in (*args, *outs))
    return pl.pallas_call(
        kernel,
        out_shape=outs,
        in_specs=[pl.BlockSpec(memory_space=pltpu.SMEM)] * len(core)
        + [whole] * len(args)
        + [left] * len(far),
        out_specs=[left] * out_far + [whole] * (len(outs) - out_far),
        scratch_shapes=list(scratch),
        compiler_params=pltpu.CompilerParams(vmem_limit_bytes=limit * 2**20),
        cost_estimate=pl.CostEstimate(flops=flops, bytes_accessed=moved, transcendentals=0),
    )(*core, *args, *far)


def scratch_like(outs):
    return [pltpu.VMEM(item.shape, item.dtype) for item in outs]


HALF = shaped((256, 512))
KEPT = (shaped((72, 256, 1024)), shaped((144, 256, 256), F32))
SAVED = (shaped((256, 1024)), HALF, HALF, HALF, shaped((8, 256, 256), F32), HALF)


def attention_forward(first, order, blocks, bias, earlier):
    outs = KEPT + (shaped((TOKENS, WIDTH)),)
    scratch = scratch_like(SAVED) + [pltpu.SemaphoreType.DMA((10,))]
    args = (first, order, *blocks, bias)
    return call(forward_kernel, outs, args, 4 * 10**9, scratch, (earlier,), 2, limit=22)


def attention_backward(projected, order, saved, earlier):
    outs = (shaped((BLOCK, 2048)),) * 4 + (shaped((TOKENS, WIDTH)), shaped((4, 256), F32))
    scratch = [
        pltpu.VMEM((2, TOKENS, 768), BF16),
        pltpu.VMEM((TOKENS, WIDTH), BF16),
        pltpu.VMEM((4, BLOCK, 2048), BF16),
        *scratch_like((shaped((2, 256, WIDTH)),) * 4 + SAVED),
        pltpu.SemaphoreType.DMA((4,)),
        pltpu.SemaphoreType.DMA((10,)),
    ]
    return call(backward_kernel, outs, (projected, order), 4 * 10**9, scratch, (*saved, earlier), 4, limit=24)


def feed_forward(second, branch, order, hidden, mine, theirs):
    wide, narrow = shaped((2, TOKENS, 2048)), shaped((TOKENS, WIDTH))
    outs = (shaped((2, TOKENS, WIDTH)), wide, narrow, narrow, shaped((1, 2048), F32))
    scratch = (
        pltpu.VMEM((2, 4, 4, 2, 16, 2048), BF16),
        pltpu.VMEM((2, 4, 4, 2, 16, 2048), BF16),
        pltpu.SemaphoreType.DMA((32,)),
    )
    args = (second, branch, order, hidden)
    return call(middle_kernel, outs, args, 6 * 10**9, scratch, (*mine, *theirs), limit=24)


def pack(inputs, plan, earlier=()):
    outs = tuple(
        shaped((sum(rows for _, _, rows in parts),) + inputs[0].shape[1:]) for parts in plan
    )
    return call(functools.partial(pack_kernel, plan), outs, tuple(inputs), 10**5, far=earlier)


def feed_forward_rows(rel, columns, theirs):
    return call(rows_kernel, (shaped((2, 128, 2048)),) * 4, (rel, columns, theirs), 10**9, limit=20)


def halves(rows):
    half = rows.shape[0] // 2
    return rows[:half], rows[half:]


def shards(
    latents,
    conditioning,
    cotangent,
    modulate_weight,
    modulate_bias,
    attend_weight,
    attend_bias,
    project_weight,
    project_bias,
    hidden_weight,
    hidden_bias,
    output_weight,
    output_bias,
):
    place = Place()
    width = conditioning.shape[1]

    modulate = modulate_weight[:, 0]
    order_a = one_hot(place.attention_order())
    order_f = one_hot(place.forward_order())

    bias_own = lax.dynamic_slice_in_dim(attend_bias[0], place.c * 256, 256, 1)
    bias_rows = jnp.pad(bias_own.reshape(1, 512), ((0, 15), (0, 512)))
    core = place.c.reshape(1).astype(jnp.int32)
    quarter = shaped((16, 1024))
    mine, theirs, forward_piece = call(
        split_kernel,
        (quarter, quarter, shaped((64, 1024))),
        (attend_weight[0], project_weight[0], hidden_weight[0], output_weight[0]),
        10**5,
        core=(core,),
    )
    piece, for_t, for_w = call(
        join_kernel,
        (shaped((32, 1024)), shaped((48, 1024)), shaped((96, 1024))),
        (mine, swap_core(theirs), forward_piece, bias_rows),
        10**5,
        core=(core,),
    )
    flipped_w = flip_x(for_w, 1, 0)
    flipped_t = flip_x(for_t, 0, 1)
    flipped_both = flip_x(piece, 1, 1)
    bias_pair = jnp.concatenate([bias_own, flipped_t[32, :512].reshape(2, 256)], axis=1).astype(F32)
    on_first = place.t == 0
    (stage_one,) = pack(
        [piece, flipped_w, flipped_t, flipped_both, forward_piece],
        [[(0, 0, 32), (1, 0, 32), (2, 0, 32), (3, 0, 32), (4, 0, 64), (1, 32, 64)]],
    )

    (moved,) = pack([latents[0], cotangent[0]], [[(0, 0, 128), (1, 0, 128)]], (stage_one,))
    moved = swap_layout(moved)
    stream, grad = moved[:128].astype(F32), moved[128:].astype(F32)

    stage_two = by_step(stage_one, {k: flip_plane(stage_one, k, False) for k in STEPS})
    attend_two, forward_two = pack(
        stage_two, [[(k, begin, 128) for k in range(4)] for begin in (0, 128)]
    )
    attend_got = [flip_plane(attend_two, k, True) for k in (1, 2, 3)]
    attend_blocks = [attend_two] + attend_got
    attend_blocks = [item.reshape(2, 256, WIDTH) for item in attend_blocks]
    forward_got = {k: flip_plane(forward_two, k, True) for k in STEPS}

    silu_rows = lax.all_to_all(
        after(conditioning, piece).reshape(64, 16), DP, 0, 0, tiled=True
    )
    silu_rows = after(silu_rows, attend_two, moved)
    silu_rows = jax.nn.silu(silu_rows.astype(F32)).astype(BF16)

    silu_chip = lax.dynamic_index_in_dim(silu_rows.reshape(32, 2, 16), place.t, 1, keepdims=False)
    terms = dot(silu_chip, modulate).reshape(64, 24, 128)
    terms = lax.all_to_all(terms, DP, 0, 0)
    mods_half = jnp.sum(terms, axis=0).reshape(3072)
    bias_row = after(modulate_bias, attend_got[1])[0].astype(F32)
    mods = lax.all_gather(mods_half, "c", axis=0, tiled=True) + bias_row
    mods = mods.reshape(6, width)

    normed_first, inverse_first = normalize(stream)
    first_in = (normed_first * (1.0 + mods[1]) + mods[0]).astype(BF16)
    first_all = jnp.concatenate([first_in, swap_core(first_in)])
    grad_branch = (grad * mods[5]).astype(BF16)
    out_bias_part = jnp.sum(grad_branch.astype(F32), axis=0)
    branch_other = swap_t(grad_branch)
    branch_all = jnp.concatenate([grad_branch, branch_other])
    *saved, partial = attention_forward(
        first_all, order_a, attend_blocks, bias_pair, forward_got[2]
    )
    own, other = halves(partial)
    projected = (
        own.astype(F32)
        + swap_core(other).astype(F32)
        + after(project_bias, forward_got[1], branch_other).astype(F32)
    )
    middle = stream + mods[2] * projected

    normed_second, inverse_second = normalize(middle)
    second_in = (normed_second * (1.0 + mods[4]) + mods[3]).astype(BF16)
    second_all = jnp.concatenate([second_in, swap_t(second_in)])
    forward_mine = [
        item.reshape(4, 2, 4, 16, 1024) for item in by_step(forward_two, forward_got)
    ]
    forward_theirs = [swap_core(item) for item in forward_mine]
    rel_pair, grad_pair, branch_partial, back_partial, hidden_bias_part = feed_forward(
        second_all, branch_all, order_f, hidden_bias.astype(F32), forward_mine, forward_theirs
    )

    def weight_grads(rows):
        return lax.dot_general(
            rows, grad_pair, (((1,), (1,)), ((0,), (0,))), preferred_element_type=F32
        )

    theirs = swap_core(weight_grads(rel_pair[:, :, 512:]).astype(BF16))
    forward_blocks = feed_forward_rows(rel_pair, grad_pair, theirs)
    forward_sent = send_plane(forward_blocks, True)
    own, other = halves(back_partial)
    branch_own, branch_other = halves(branch_partial)
    received = swap_t(jnp.concatenate([other, branch_other]))
    grad_second = own.astype(F32) + received[:128].astype(F32)
    scale_second = after(mods[4:5], *forward_blocks[1:])
    grad_shift_second = jnp.sum(grad_second, axis=0)
    grad_scale_second = jnp.sum(grad_second * normed_second, axis=0)
    grad_middle = grad + normalize_back(
        grad_second * (1.0 + scale_second), normed_second, inverse_second
    )

    grad_gate_first = jnp.sum(grad_middle * projected, axis=0)
    grad_projected = (grad_middle * mods[2]).astype(BF16)
    project_bias_part = jnp.sum(grad_projected.astype(F32), axis=0)
    projected_all = jnp.concatenate([grad_projected, swap_core(grad_projected)])
    *attend_grads, partial, attend_bias_part = attention_backward(
        projected_all,
        order_a,
        saved,
        forward_sent[2],
    )
    attend_sent = send_plane(attend_grads, True)
    branch = branch_own.astype(F32) + received[128:].astype(F32) + output_bias[0].astype(F32)
    grad_gate_second = jnp.sum(grad * branch, axis=0)
    own, other = halves(partial)
    grad_first = own.astype(F32) + swap_core(other).astype(F32)
    scale_first = after(mods[1:2], partial, forward_sent[1], forward_sent[3])
    attend_bias_part = attend_bias_part.reshape(2, 2, 256)
    attend_bias_part = jnp.where(on_first, attend_bias_part, attend_bias_part[::-1])
    grad_shift_first = jnp.sum(grad_first, axis=0)
    grad_scale_first = jnp.sum(grad_first * normed_first, axis=0)
    grad_stream = grad_middle + normalize_back(
        grad_first * (1.0 + scale_first), normed_first, inverse_first
    )
    sums = jnp.concatenate(
        [
            jnp.stack([grad_shift_first, grad_scale_first, grad_gate_first]).reshape(2, 1536),
            jnp.stack([grad_shift_second, grad_scale_second, grad_gate_second]).reshape(2, 1536),
        ],
        axis=0,
    ).reshape(2, 3072)
    sums = jnp.concatenate(
        [
            sums,
            out_bias_part.reshape(2, 512),
            project_bias_part.reshape(2, 512),
            hidden_bias_part.reshape(2, 1024),
        ],
        axis=1,
    )
    sums = lax.dynamic_index_in_dim(sums, place.c, 0, keepdims=False) + swap_core(
        lax.dynamic_index_in_dim(sums, 1 - place.c, 0, keepdims=False)
    )
    sums = after(sums.reshape(40, 128), attend_sent[2]).reshape(5120)
    mod_low = sums[:3072].astype(BF16)
    hidden_sum = sums[4096:]
    biases = jnp.concatenate(
        [
            sums[3072:4096],
            jnp.where(on_first, hidden_sum, 0.0),
            jnp.where(on_first, 0.0, hidden_sum),
            attend_bias_part.reshape(1024),
        ]
    ).astype(BF16)
    chunks = jnp.broadcast_to(biases.reshape(32, 1, 128), (32, 2, 128)).reshape(64, 128)
    payload = jnp.concatenate(
        [jnp.broadcast_to(mod_low.reshape(24, 128), (64, 24, 128)), chunks[:, None]], axis=1
    )
    payload = lax.all_to_all(payload, CHIPS, 0, 0)

    blocks_two = call(
        join_sums_kernel,
        (shaped((128, 2048)),) * 4,
        (*by_step(attend_grads[0], attend_sent), *by_step(forward_blocks[0], forward_sent)),
        10**6,
        limit=24,
    )
    bias_chunk = jnp.sum(payload[:, 24].astype(F32), axis=0)
    mod_mine = payload[:, :24].reshape(64, 3072)
    mod_theirs = swap_core(mod_mine)
    mod_all = jnp.where(
        place.first,
        jnp.concatenate([mod_mine, mod_theirs], axis=1),
        jnp.concatenate([mod_theirs, mod_mine], axis=1),
    )
    grad_ada = dot_tn(silu_rows, mod_all)[:, None]
    ada_bias_sum = jnp.sum(mod_all.astype(F32), axis=0)[None]
    row_parts = dot_nt(mod_all, modulate)
    payload = jnp.stack(
        [jnp.pad(row_parts, ((0, 0), (0, 112))), jnp.broadcast_to(bias_chunk, (64, 128))], axis=1
    )
    row_payload = after(payload, blocks_two[0])
    payload = lax.all_to_all(row_payload, DP, 0, 0)
    grad_silu = payload[:, 0, :16].reshape(1, width)
    _, silu_back = jax.vjp(jax.nn.silu, conditioning.astype(F32))
    grad_conditioning = silu_back(grad_silu)[0].astype(BF16)
    bias_sums = payload[:, 1].reshape(32, 2, 128).transpose(1, 0, 2).reshape(2, 4096)
    out_bias_sum = bias_sums[:, :512].reshape(1, 1024)
    project_bias_sum = bias_sums[:, 512:1024].reshape(1, 1024)
    hidden_bias_sum = lax.dynamic_index_in_dim(
        bias_sums[:, 1024:3072].reshape(2, 2, 1024), place.t, 1, keepdims=False
    ).reshape(1, 2048)
    attend_bias_sum = lax.dynamic_index_in_dim(
        bias_sums[:, 3072:].reshape(2, 2, 2, 256), place.t, 1, keepdims=False
    )
    attend_bias_sum = attend_bias_sum.transpose(1, 0, 2).reshape(1, 2, 512)

    sent_two = send_plane(blocks_two, False)
    flips = ((0, 0), (0, 1), (1, 0), (1, 1))
    attend_own, forward_own, *attend_rest = call(
        last_sums_kernel,
        (shaped((32, 1024), F32), shaped((2, 16, 2048), F32), shaped((32, 1024)),
         shaped((96, 1024)), shaped((32, 1024))),
        tuple(by_step(blocks_two[0], sent_two)),
        10**6,
        far=(row_payload,),
    )
    gate_second = after(mods[5:6], attend_own)
    block_low = (middle + gate_second * branch).astype(BF16)
    moved = swap_layout(jnp.stack([block_low, grad_stream.astype(BF16)]))
    block_output, grad_latents = moved[:1], moved[1:]
    flipped_t, flipped_w, flipped_both = (
        flip_x(item, w, t) for item, (w, t) in zip(attend_rest, flips[1:])
    )
    forward_other = flipped_w[32:].reshape(2, 2, 16, 1024).transpose(0, 2, 1, 3)
    forward_grads = forward_own + forward_other.reshape(2, 16, 2048).astype(F32)
    reduced = add_up(attend_own, [flipped_t, flipped_w[:32], flipped_both]).reshape(2, 16, 1024)
    mine = lax.dynamic_index_in_dim(reduced, place.c, 0, keepdims=False)
    theirs = swap_core(lax.dynamic_index_in_dim(reduced, 1 - place.c, 0, keepdims=False))
    low = jnp.where(place.first, mine, theirs).reshape(16, 4, 256)
    high = jnp.where(place.first, theirs, mine).reshape(16, 4, 256)
    reduced = jnp.concatenate([low, high], axis=2)


    return (
        block_output,
        grad_latents,
        grad_conditioning,
        grad_ada,
        ada_bias_sum,
        reduced[None, :, :3],
        attend_bias_sum,
        reduced[None, :, 3],
        project_bias_sum,
        forward_grads[0][None],
        hidden_bias_sum,
        forward_grads[1][None],
        out_bias_sum,
    )


def solution(mesh):
    fine = Mesh(mesh.devices.reshape(4, 2, 4, 2, 2), ("z", "w", "y", "c", "t"))
    return jax.shard_map(
        shards,
        mesh=fine,
        in_specs=(
            P(DP, "t", None),
            P(DP, None),
            P(DP, "t", None),
            P(DP, None, None),
            P(),
            P(None, DP, None, "t"),
            P(None, None, "t"),
            P(None, DP, "t"),
            P(),
            P(None, DP, "t"),
            P(None, "t"),
            P(None, DP, "t"),
            P(),
        ),
        out_specs=(
            P(DP, "t", None),
            P(DP, "t", None),
            P(DP, None),
            P(DP, None, None),
            P(),
            P(None, DP, None, "t"),
            P(None, None, "t"),
            P(None, DP, "t"),
            P(),
            P(None, DP, "t"),
            P(None, "t"),
            P(None, DP, "t"),
            P(),
        ),
        check_vma=False,
    )
```

```python
import functools
import math

import jax
import jax.numpy as jnp
from jax import lax
from jax.experimental import pallas as pl
from jax.experimental.pallas import tpu as pltpu
from jax.sharding import Mesh
from jax.sharding import PartitionSpec as P

HEAD_DIM = 64
EPS = 1e-06
F32 = jnp.float32
BF16 = jnp.bfloat16
DP = ("z", "w", "y", "c")
CHIPS = ("z", "w", "y", "t")


def normalize(values):
    centered = values - jnp.mean(values, axis=-1, keepdims=True)
    inverse = lax.rsqrt(jnp.mean(centered * centered, axis=-1, keepdims=True) + EPS)
    return (centered * inverse, inverse)


def normalize_back(grad, normed, inverse):
    return inverse * (
        grad
        - jnp.mean(grad, axis=-1, keepdims=True)
        - normed * jnp.mean(grad * normed, axis=-1, keepdims=True)
    )


def dot(left, right):
    return jnp.dot(left, right, preferred_element_type=F32)


def dot_nt(left, right):
    return lax.dot_general(left, right, (((1,), (1,)), ((), ())), preferred_element_type=F32)


def dot_tn(left, right):
    return lax.dot_general(left, right, (((0,), (0,)), ((), ())), preferred_element_type=F32)


def swap_core(piece):
    return lax.ppermute(piece, "c", [(0, 1), (1, 0)])


def swap_t(piece):
    return lax.ppermute(piece, "t", [(0, 1), (1, 0)])


def swap_layout(piece):
    return lax.ppermute(piece, ("c", "t"), [(0, 0), (1, 2), (2, 1), (3, 3)])


def flip_plane(piece, step, last):
    perm = []
    for z in range(4):
        for y in range(4):
            for c in range(2):
                along_z = (c == 0) == last
                z2, y2 = (z ^ step, y) if along_z else (z, y ^ step)
                perm.append(((z * 4 + y) * 2 + c, (z2 * 4 + y2) * 2 + c))
    return lax.ppermute(piece, ("z", "y", "c"), perm)


def flip_x(piece, w_step, t_step):
    perm = [(w * 2 + t, (w ^ w_step) * 2 + (t ^ t_step)) for w in range(2) for t in range(2)]
    return lax.ppermute(piece, ("w", "t"), perm)


STEPS = (2, 1, 3)


def after(value, *others):
    def copy(source, *rest):
        rest[-1][...] = source[...]

    whole = pl.BlockSpec(memory_space=pltpu.VMEM)
    left = pl.BlockSpec(memory_space=pl.ANY)
    return pl.pallas_call(
        copy,
        out_shape=jax.ShapeDtypeStruct(value.shape, value.dtype),
        in_specs=[whole] + [left] * len(others),
        out_specs=whole,
    )(value, *others)


def by_step(own, received):
    return [own] + [received[k] for k in (1, 2, 3)]


def one_hot(order):
    features = lax.broadcasted_iota(jnp.int32, (1024, 1024), 0)
    return (features == order[None, :]).astype(BF16)


class Place:
    def __init__(self):
        self.z = lax.axis_index("z")
        self.w = lax.axis_index("w")
        self.y = lax.axis_index("y")
        self.c = lax.axis_index("c")
        self.t = lax.axis_index("t")
        self.first = self.c == 0

    def attention_order(self):
        place = lax.iota(jnp.int32, 1024)
        last, before, w_step, row = place // 256, place // 64 % 4, place // 32 % 2, place % 32
        z = self.z ^ jnp.where(self.first, last, before)
        y = self.y ^ jnp.where(self.first, before, last)
        return ((z * 2 + (self.w ^ w_step)) * 4 + y) * 32 + row

    def forward_order(self):
        place = lax.iota(jnp.int32, 1024)
        core = self.c ^ (place // 512)
        last, before, w_step, row = place // 128 % 4, place // 32 % 4, place // 16 % 2, place % 16
        z = self.z ^ jnp.where(core == 0, last, before)
        y = self.y ^ jnp.where(core == 0, before, last)
        return ((z * 2 + (self.w ^ w_step)) * 4 + y) * 32 + core * 16 + row


def add_up(own, received):
    total = own.astype(F32)
    for block in received:
        total = total + block.astype(F32)
    return total


def send_plane(blocks, last):
    return {k: flip_plane(blocks[k], k, last) for k in STEPS}


def reduce_plane(blocks, last):
    return add_up(blocks[0], send_plane(blocks, last).values())


TOKENS = 256
WIDTH = 1024
BLOCK = 256
ALL_HEADS = [(t, h) for t in range(2) for h in range(4)]
SCALE = HEAD_DIM ** (-0.5)


def head_columns(t, h):
    return slice(t * 256 + h * HEAD_DIM, t * 256 + (h + 1) * HEAD_DIM)


def weight_rows(block, t, columns):
    rows = [block[k // 2, (k % 2) * 128 + t * 64 : (k % 2) * 128 + (t + 1) * 64, columns] for k in range(4)]
    return jnp.concatenate(rows)


TRIPLE, PROJECT = slice(0, 768), slice(768, 1024)


def places(kept, kept_probs):
    left, right = pl.ds(0, 512), pl.ds(512, 512)
    return (
        kept.at[0],
        kept.at[1, :, left],
        kept.at[1, :, right],
        kept.at[2, :, left],
        kept_probs.at[pl.ds(0, 8)],
        kept.at[2, :, right],
        *(kept.at[pl.ds(4 + 2 * k, 2)] for k in range(4)),
    )


def forward_kernel(
    first, order, w0, w1, w2, w3, bias, one,
    kept, kept_probs, out, rel, query, key, value, probs, mixed, sent,
):
    blocks = (w0, w1, w2, w3)
    copies = [
        pltpu.make_async_copy(source, target, sent.at[i])
        for i, (source, target) in enumerate(
            zip((rel, query, key, value, probs, mixed, *blocks), places(kept, kept_probs))
        )
    ]
    for copy in copies[6:]:
        copy.start()
    rel[...] = dot(first[...], order[...]).astype(BF16)
    copies[0].start()
    for t in range(2):
        packed = sum(
            dot(rel[:, k * BLOCK : (k + 1) * BLOCK], weight_rows(blocks[k], t, TRIPLE))
            for k in range(4)
        )
        columns = slice(t * 256, (t + 1) * 256)
        query[:, columns] = (packed[:, :256] + bias[0:1, columns]).astype(BF16)
        key[:, columns] = packed[:, 256:512].astype(BF16)
        value[:, columns] = (packed[:, 512:768] + bias[1:2, columns]).astype(BF16)
    for copy in copies[1:4]:
        copy.start()
    for t, h in ALL_HEADS:
        columns = head_columns(t, h)
        scores = dot_nt(query[:, columns], key[:, columns]) * SCALE
        expd = jnp.exp(scores - jnp.max(scores, axis=-1, keepdims=True))
        prob = expd / jnp.sum(expd, axis=-1, keepdims=True)
        probs[t * 4 + h] = prob
        mixed[:, columns] = dot(prob.astype(BF16), value[:, columns]).astype(BF16)
    for copy in copies[4:6]:
        copy.start()
    partial = [
        sum(
            dot_nt(mixed[:, t * 256 : (t + 1) * 256], weight_rows(blocks[k], t, PROJECT))
            for t in range(2)
        ).astype(BF16)
        for k in range(4)
    ]
    out[...] = dot_nt(jnp.concatenate(partial, axis=1), order[...]).astype(BF16)
    for copy in copies:
        copy.wait()


def backward_kernel(
    projected, order, kept, kept_probs, one, g0, g1, g2, g3, out, bias,
    packed, back, ready, w0, w1, w2, w3, rel, query, key, value, probs, mixed, sent, arrived,
):
    blocks = (w0, w1, w2, w3)
    fetched = [
        pltpu.make_async_copy(source, target, arrived.at[i])
        for i, (source, target) in enumerate(
            zip(
                places(kept, kept_probs),
                (rel, query, key, value, probs, mixed, w0, w1, w2, w3),
            )
        )
    ]
    for copy in fetched:
        copy.start()
    copies = [
        pltpu.make_async_copy(ready.at[k], target, sent.at[k])
        for k, target in enumerate((g0, g1, g2, g3))
    ]
    back[...] = dot(projected[...], order[...]).astype(BF16)
    for copy in fetched:
        copy.wait()
    for t in range(2):
        grad_mixed = sum(
            dot(back[:, k * BLOCK : (k + 1) * BLOCK], weight_rows(blocks[k], t, PROJECT))
            for k in range(4)
        ).astype(BF16)
        for h in range(4):
            columns = head_columns(t, h)
            grad_head = grad_mixed[:, h * HEAD_DIM : (h + 1) * HEAD_DIM]
            prob = probs[t * 4 + h]
            grad_value = dot_tn(prob.astype(BF16), grad_head)
            grad_probs = dot_nt(grad_head, value[:, columns])
            grad_scores = (
                prob * (grad_probs - jnp.sum(grad_probs * prob, axis=-1, keepdims=True))
            ).astype(BF16)
            grad_query = dot(grad_scores, key[:, columns]) * SCALE
            grad_key = dot_tn(grad_scores, query[:, columns]) * SCALE
            for i, item in enumerate((grad_query, grad_key, grad_value)):
                begin = i * 256 + h * HEAD_DIM
                packed[t, :, begin : begin + HEAD_DIM] = item.astype(BF16)
        for row, begin in enumerate((0, 512)):
            bias[t * 2 + row : t * 2 + row + 1, :] = jnp.sum(
                packed[t, :, begin : begin + 256].astype(F32), axis=0, keepdims=True
            )
    partial = []
    for k in range(4):
        rows = slice(k * BLOCK, (k + 1) * BLOCK)
        for t in range(2):
            ready[k, :, t * 1024 : t * 1024 + 768] = dot_tn(rel[:, rows], packed[t]).astype(BF16)
            ready[k, :, t * 1024 + 768 : (t + 1) * 1024] = dot_tn(
                back[:, rows], mixed[:, t * 256 : (t + 1) * 256]
            ).astype(BF16)
        copies[k].start()
        partial.append(
            sum(dot_nt(packed[t], weight_rows(blocks[k], t, TRIPLE)) for t in range(2)).astype(BF16)
        )
    out[...] = dot_nt(jnp.concatenate(partial, axis=1), order[...]).astype(BF16)
    for copy in copies:
        copy.wait()


def middle_kernel(
    second, branch, order, hidden, m0, m1, m2, m3, t0, t1, t2, t3,
    rel, active, out, back, hidden_sum, mine, theirs, arrived,
):
    copies = []
    for which in range(2):
        for half in range(2):
            for target, blocks in ((mine, (m0, m1, m2, m3)), (theirs, (t0, t1, t2, t3))):
                for k, block in enumerate(blocks):
                    copies.append(
                        pltpu.make_async_copy(
                            block.at[:, :, which * 2 + half],
                            target.at[which, k, :, :, :, pl.ds(half * 1024, 1024)],
                            arrived.at[len(copies)],
                        )
                    )
    for copy in copies:
        copy.start()
    rel[0] = dot(second[...], order[...]).astype(BF16)
    rel[1] = dot(branch[...], order[...]).astype(BF16)
    for copy in copies:
        copy.wait()

    def rows(source, which, columns):
        return source[which, :, :, :, :, columns].reshape(512, columns.stop - columns.start)

    root = (2.0 / math.pi) ** 0.5
    for begin in range(0, 2048, 512):
        columns = slice(begin, begin + 512)
        pre = (
            dot(rel[0, :, :512], rows(mine, 0, columns))
            + dot(rel[0, :, 512:], rows(theirs, 0, columns))
            + hidden[0:1, columns]
        )
        grad_active = dot(rel[1, :, :512], rows(mine, 1, columns)) + dot(
            rel[1, :, 512:], rows(theirs, 1, columns)
        )
        square = pre * pre
        bent = jnp.tanh(root * (pre + 0.044715 * (square * pre)))
        half = 0.5 * (1.0 + bent)
        active[1, :, columns] = (pre * half).astype(BF16)
        slope = half + (0.5 * pre) * (1.0 - bent * bent) * (root * (1.0 + 0.134145 * square))
        low = (grad_active * slope).astype(BF16)
        active[0, :, columns] = low
        hidden_sum[0:1, columns] = jnp.sum(low.astype(F32), axis=0, keepdims=True)
    for which, target in ((0, back), (1, out)):
        partial = jnp.concatenate(
            [
                dot_nt(active[which], rows(item, which, slice(0, 2048))).astype(BF16)
                for item in (mine, theirs)
            ],
            axis=1,
        )
        target[...] = dot_nt(partial, order[...]).astype(BF16)


def rows_kernel(rel, columns, theirs, *outs):
    for k, out in enumerate(outs):
        rows = slice(k * 128, (k + 1) * 128)
        for which in range(2):
            out[which] = (
                dot_tn(rel[which, :, rows], columns[which]) + theirs[which, rows].astype(F32)
            ).astype(BF16)


def total_of(blocks, *index):
    return sum(block[index].astype(F32) for block in blocks)


def join_sums_kernel(*refs):
    attend, forward, outs = refs[:4], refs[4:8], refs[-4:]
    for k, out in enumerate(outs):
        out[0:64] = total_of(attend, slice(k * 64, (k + 1) * 64)).astype(BF16)
        for which in range(2):
            rows = slice(k * 32, (k + 1) * 32)
            out[64 + which * 32 : 96 + which * 32] = total_of(forward, which, rows).astype(BF16)


def last_sums_kernel(b0, b1, b2, b3, one, two, three, attend_own, forward_own, for_t, for_w, for_both):
    blocks = (b0, b1, b2, b3)
    low, high = slice(0, 1024), slice(1024, 2048)
    attend_own[...] = total_of(blocks, slice(0, 32), low)
    for_t[...] = total_of(blocks, slice(0, 32), high).astype(BF16)
    for_w[0:32] = total_of(blocks, slice(32, 64), low).astype(BF16)
    for_both[...] = total_of(blocks, slice(32, 64), high).astype(BF16)
    for which in range(2):
        begin = 64 + which * 32
        forward_own[which] = total_of(blocks, slice(begin, begin + 16))
        for half, columns in enumerate((low, high)):
            at = 32 + (which * 2 + half) * 16
            for_w[at : at + 16] = total_of(blocks, slice(begin + 16, begin + 32), columns).astype(
                BF16
            )


def split_kernel(core, attend, project, hidden, output, mine, theirs, forward, held, arrived):
    copies = [pltpu.make_async_copy(project, held, arrived.at[4])]
    for which, source in enumerate((hidden, output)):
        for half in range(2):
            piece = which * 2 + half
            copies.append(
                pltpu.make_async_copy(
                    source.at[:, pl.ds(half * 1024, 1024)],
                    forward.at[pl.ds(piece * 16, 16)],
                    arrived.at[piece],
                )
            )
    for copy in copies:
        copy.start()
    first = core[0] == 0

    def split(j, rows):
        low, high = rows[:, :256], rows[:, 256:]
        mine[:, j * 256 : (j + 1) * 256] = jnp.where(first, low, high)
        theirs[:, j * 256 : (j + 1) * 256] = jnp.where(first, high, low)

    for j in range(3):
        split(j, attend[:, j, :])
    for copy in copies:
        copy.wait()
    split(3, held[...])


def join_kernel(core, mine, theirs, forward, bias, piece, for_t, for_w):
    first = core[0] == 0
    for target in (piece, for_t, for_w):
        target[0:16] = jnp.where(first, mine[...], theirs[...])
        target[16:32] = jnp.where(first, theirs[...], mine[...])
    for_t[32:48] = bias[...]
    for_w[32:96] = forward[...]


def bias_kernel(t, sums, out, project, hidden, attend):
    on_first = t[0] == 0

    def chunk(j, core):
        return sums[j * 2 + core : j * 2 + core + 1]

    for core in range(2):
        for i in range(4):
            columns = slice(core * 512 + i * 128, core * 512 + (i + 1) * 128)
            out[:, columns] = chunk(i, core)
            project[:, columns] = chunk(4 + i, core)
        for i in range(8):
            columns = slice(core * 1024 + i * 128, core * 1024 + (i + 1) * 128)
            hidden[:, columns] = jnp.where(on_first, chunk(8 + i, core), chunk(16 + i, core))
        for i in range(4):
            begin = core * 256 + i % 2 * 128
            attend[0, i // 2 : i // 2 + 1, begin : begin + 128] = jnp.where(
                on_first, chunk(24 + i, core), chunk(28 + i, core)
            )


def part_kernel(source, one, mods, biases):
    mods[...] = source[:, 0:24]
    biases[...] = source[:, 24].astype(F32)


def pack_kernel(plan, *refs):
    outs = refs[len(refs) - len(plan) :]
    for out, parts in zip(outs, plan):
        at = 0
        for source, begin, rows in parts:
            out[at : at + rows] = refs[source][begin : begin + rows]
            at += rows


def shaped(shape, kind=BF16):
    return jax.ShapeDtypeStruct(shape, kind)


def call(kernel, outs, args, flops, scratch=(), far=(), out_far=0, core=(), limit=12):
    whole = pl.BlockSpec(memory_space=pltpu.VMEM)
    left = pl.BlockSpec(memory_space=pl.ANY)
    moved = sum(item.size * item.dtype.itemsize for item in (*args, *outs))
    return pl.pallas_call(
        kernel,
        out_shape=outs,
        in_specs=[pl.BlockSpec(memory_space=pltpu.SMEM)] * len(core)
        + [whole] * len(args)
        + [left] * len(far),
        out_specs=[left] * out_far + [whole] * (len(outs) - out_far),
        scratch_shapes=list(scratch),
        compiler_params=pltpu.CompilerParams(vmem_limit_bytes=limit * 2**20),
        cost_estimate=pl.CostEstimate(flops=flops, bytes_accessed=moved, transcendentals=0),
    )(*core, *args, *far)


def scratch_like(outs):
    return [pltpu.VMEM(item.shape, item.dtype) for item in outs]


HALF = shaped((256, 512))
KEPT = (shaped((72, 256, 1024)), shaped((144, 256, 256), F32))
SAVED = (shaped((256, 1024)), HALF, HALF, HALF, shaped((8, 256, 256), F32), HALF)


def attention_forward(first, order, blocks, bias, earlier):
    outs = KEPT + (shaped((TOKENS, WIDTH)),)
    scratch = scratch_like(SAVED) + [pltpu.SemaphoreType.DMA((10,))]
    args = (first, order, *blocks, bias)
    return call(forward_kernel, outs, args, 4 * 10**9, scratch, (earlier,), 2, limit=22)


def attention_backward(projected, order, saved, earlier):
    outs = (shaped((BLOCK, 2048)),) * 4 + (shaped((TOKENS, WIDTH)), shaped((4, 256), F32))
    scratch = [
        pltpu.VMEM((2, TOKENS, 768), BF16),
        pltpu.VMEM((TOKENS, WIDTH), BF16),
        pltpu.VMEM((4, BLOCK, 2048), BF16),
        *scratch_like((shaped((2, 256, WIDTH)),) * 4 + SAVED),
        pltpu.SemaphoreType.DMA((4,)),
        pltpu.SemaphoreType.DMA((10,)),
    ]
    return call(backward_kernel, outs, (projected, order), 4 * 10**9, scratch, (*saved, earlier), 4, limit=24)


def feed_forward(second, branch, order, hidden, mine, theirs):
    wide, narrow = shaped((2, TOKENS, 2048)), shaped((TOKENS, WIDTH))
    outs = (shaped((2, TOKENS, WIDTH)), wide, narrow, narrow, shaped((1, 2048), F32))
    scratch = (
        pltpu.VMEM((2, 4, 4, 2, 16, 2048), BF16),
        pltpu.VMEM((2, 4, 4, 2, 16, 2048), BF16),
        pltpu.SemaphoreType.DMA((32,)),
    )
    args = (second, branch, order, hidden)
    return call(middle_kernel, outs, args, 6 * 10**9, scratch, (*mine, *theirs), limit=24)


def pack(inputs, plan, earlier=()):
    outs = tuple(
        shaped((sum(rows for _, _, rows in parts),) + inputs[0].shape[1:]) for parts in plan
    )
    return call(functools.partial(pack_kernel, plan), outs, tuple(inputs), 10**5, far=earlier)


def feed_forward_rows(rel, columns, theirs):
    return call(rows_kernel, (shaped((2, 128, 2048)),) * 4, (rel, columns, theirs), 10**9, limit=20)


def halves(rows):
    half = rows.shape[0] // 2
    return rows[:half], rows[half:]


def shards(
    latents,
    conditioning,
    cotangent,
    modulate_weight,
    modulate_bias,
    attend_weight,
    attend_bias,
    project_weight,
    project_bias,
    hidden_weight,
    hidden_bias,
    output_weight,
    output_bias,
):
    place = Place()
    width = conditioning.shape[1]

    modulate = modulate_weight[:, 0]
    order_a = one_hot(place.attention_order())
    order_f = one_hot(place.forward_order())

    bias_own = lax.dynamic_slice_in_dim(attend_bias[0], place.c * 256, 256, 1)
    bias_rows = jnp.pad(bias_own.reshape(1, 512), ((0, 15), (0, 512)))
    core = place.c.reshape(1).astype(jnp.int32)
    quarter = shaped((16, 1024))
    mine, theirs, forward_piece = call(
        split_kernel,
        (quarter, quarter, shaped((64, 1024))),
        (attend_weight[0],),
        10**5,
        (pltpu.VMEM((16, 512), BF16), pltpu.SemaphoreType.DMA((5,))),
        (project_weight[0], hidden_weight[0], output_weight[0]),
        core=(core,),
    )
    piece, for_t, for_w = call(
        join_kernel,
        (shaped((32, 1024)), shaped((48, 1024)), shaped((96, 1024))),
        (mine, swap_core(theirs), forward_piece, bias_rows),
        10**5,
        core=(core,),
    )
    flipped_w = flip_x(for_w, 1, 0)
    flipped_t = flip_x(for_t, 0, 1)
    flipped_both = flip_x(piece, 1, 1)
    bias_pair = jnp.concatenate([bias_own, flipped_t[32, :512].reshape(2, 256)], axis=1).astype(F32)
    on_first = place.t == 0
    (stage_one,) = pack(
        [piece, flipped_w, flipped_t, flipped_both, forward_piece],
        [[(0, 0, 32), (1, 0, 32), (2, 0, 32), (3, 0, 32), (4, 0, 64), (1, 32, 64)]],
    )

    (moved,) = pack([latents[0], cotangent[0]], [[(0, 0, 128), (1, 0, 128)]], (stage_one,))
    moved = swap_layout(moved)
    stream, grad = moved[:128].astype(F32), moved[128:].astype(F32)

    stage_two = by_step(stage_one, {k: flip_plane(stage_one, k, False) for k in STEPS})
    attend_two, forward_two = pack(
        stage_two, [[(k, begin, 128) for k in range(4)] for begin in (0, 128)]
    )
    attend_got = [flip_plane(attend_two, k, True) for k in (1, 2, 3)]
    attend_blocks = [attend_two] + attend_got
    attend_blocks = [item.reshape(2, 256, WIDTH) for item in attend_blocks]
    forward_got = {k: flip_plane(forward_two, k, True) for k in STEPS}

    silu_rows = lax.all_to_all(
        after(conditioning, piece).reshape(64, 16), DP, 0, 0, tiled=True
    )
    silu_rows = after(silu_rows, attend_two, moved)
    silu_rows = jax.nn.silu(silu_rows.astype(F32)).astype(BF16)

    silu_chip = lax.dynamic_index_in_dim(silu_rows.reshape(32, 2, 16), place.t, 1, keepdims=False)
    terms = dot(silu_chip, modulate).reshape(64, 24, 128)
    terms = lax.all_to_all(terms, DP, 0, 0)
    mods_half = jnp.sum(terms, axis=0).reshape(3072)
    bias_row = after(modulate_bias, attend_got[1])[0].astype(F32)
    mods = lax.all_gather(mods_half, "c", axis=0, tiled=True) + bias_row
    mods = mods.reshape(6, width)

    normed_first, inverse_first = normalize(stream)
    first_in = (normed_first * (1.0 + mods[1]) + mods[0]).astype(BF16)
    first_all = jnp.concatenate([first_in, swap_core(first_in)])
    grad_branch = (grad * mods[5]).astype(BF16)
    out_bias_part = jnp.sum(grad_branch.astype(F32), axis=0)
    branch_other = swap_t(grad_branch)
    branch_all = jnp.concatenate([grad_branch, branch_other])
    *saved, partial = attention_forward(
        first_all, order_a, attend_blocks, bias_pair, forward_got[2]
    )
    own, other = halves(partial)
    projected = (
        own.astype(F32)
        + swap_core(other).astype(F32)
        + after(project_bias, forward_got[1], branch_other).astype(F32)
    )
    middle = stream + mods[2] * projected

    normed_second, inverse_second = normalize(middle)
    second_in = (normed_second * (1.0 + mods[4]) + mods[3]).astype(BF16)
    second_all = jnp.concatenate([second_in, swap_t(second_in)])
    forward_mine = [
        item.reshape(4, 2, 4, 16, 1024) for item in by_step(forward_two, forward_got)
    ]
    forward_theirs = [swap_core(item) for item in forward_mine]
    rel_pair, grad_pair, branch_partial, back_partial, hidden_bias_part = feed_forward(
        second_all, branch_all, order_f, hidden_bias.astype(F32), forward_mine, forward_theirs
    )

    def weight_grads(rows):
        return lax.dot_general(
            rows, grad_pair, (((1,), (1,)), ((0,), (0,))), preferred_element_type=F32
        )

    theirs = swap_core(weight_grads(rel_pair[:, :, 512:]).astype(BF16))
    forward_blocks = feed_forward_rows(rel_pair, grad_pair, theirs)
    forward_sent = send_plane(forward_blocks, True)
    own, other = halves(back_partial)
    branch_own, branch_other = halves(branch_partial)
    received = swap_t(jnp.concatenate([other, branch_other]))
    grad_second = own.astype(F32) + received[:128].astype(F32)
    scale_second = after(mods[4:5], *forward_blocks[1:])
    grad_shift_second = jnp.sum(grad_second, axis=0)
    grad_scale_second = jnp.sum(grad_second * normed_second, axis=0)
    grad_middle = grad + normalize_back(
        grad_second * (1.0 + scale_second), normed_second, inverse_second
    )

    grad_gate_first = jnp.sum(grad_middle * projected, axis=0)
    grad_projected = (grad_middle * mods[2]).astype(BF16)
    project_bias_part = jnp.sum(grad_projected.astype(F32), axis=0)
    projected_all = jnp.concatenate([grad_projected, swap_core(grad_projected)])
    *attend_grads, partial, attend_bias_part = attention_backward(
        projected_all,
        order_a,
        saved,
        forward_sent[1],
    )
    attend_sent = send_plane(attend_grads, True)
    branch = branch_own.astype(F32) + received[128:].astype(F32) + output_bias[0].astype(F32)
    grad_gate_second = jnp.sum(grad * branch, axis=0)
    own, other = halves(partial)
    grad_first = own.astype(F32) + swap_core(other).astype(F32)
    scale_first = after(mods[1:2], partial, forward_sent[2], forward_sent[3])
    attend_bias_part = attend_bias_part.reshape(2, 2, 256)
    attend_bias_part = jnp.where(on_first, attend_bias_part, attend_bias_part[::-1])
    grad_shift_first = jnp.sum(grad_first, axis=0)
    grad_scale_first = jnp.sum(grad_first * normed_first, axis=0)
    grad_stream = grad_middle + normalize_back(
        grad_first * (1.0 + scale_first), normed_first, inverse_first
    )
    sums = jnp.concatenate(
        [
            jnp.stack([grad_shift_first, grad_scale_first, grad_gate_first]).reshape(2, 1536),
            jnp.stack([grad_shift_second, grad_scale_second, grad_gate_second]).reshape(2, 1536),
        ],
        axis=0,
    ).reshape(2, 3072)
    sums = jnp.concatenate(
        [
            sums,
            out_bias_part.reshape(2, 512),
            project_bias_part.reshape(2, 512),
            hidden_bias_part.reshape(2, 1024),
        ],
        axis=1,
    )
    sums = lax.dynamic_index_in_dim(sums, place.c, 0, keepdims=False) + swap_core(
        lax.dynamic_index_in_dim(sums, 1 - place.c, 0, keepdims=False)
    )
    sums = after(sums.reshape(40, 128), attend_sent[2]).reshape(5120)
    mod_low = sums[:3072].astype(BF16)
    hidden_sum = sums[4096:]
    biases = jnp.concatenate(
        [
            sums[3072:4096],
            jnp.where(on_first, hidden_sum, 0.0),
            jnp.where(on_first, 0.0, hidden_sum),
            attend_bias_part.reshape(1024),
        ]
    ).astype(BF16)
    chunks = jnp.broadcast_to(biases.reshape(32, 1, 128), (32, 2, 128)).reshape(64, 128)
    payload = jnp.concatenate(
        [jnp.broadcast_to(mod_low.reshape(24, 128), (64, 24, 128)), chunks[:, None]], axis=1
    )
    payload = lax.all_to_all(payload, CHIPS, 0, 0)

    blocks_two = call(
        join_sums_kernel,
        (shaped((128, 2048)),) * 4,
        (*by_step(attend_grads[0], attend_sent), *by_step(forward_blocks[0], forward_sent)),
        10**6,
        limit=24,
    )
    mod_mine, bias_rows = call(
        part_kernel,
        (shaped((64, 24, 128)), shaped((64, 128), F32)),
        (payload,),
        10**5,
        far=(blocks_two[0],),
    )
    bias_chunk = jnp.sum(bias_rows, axis=0)
    mod_mine = mod_mine.reshape(64, 3072)
    mod_theirs = swap_core(mod_mine)
    mod_all = jnp.where(
        place.first,
        jnp.concatenate([mod_mine, mod_theirs], axis=1),
        jnp.concatenate([mod_theirs, mod_mine], axis=1),
    )
    grad_ada = dot_tn(silu_rows, mod_all)[:, None]
    ada_bias_sum = jnp.sum(mod_all.astype(F32), axis=0)[None]
    row_parts = dot_nt(mod_all, modulate)
    payload = jnp.stack(
        [jnp.pad(row_parts, ((0, 0), (0, 112))), jnp.broadcast_to(bias_chunk, (64, 128))], axis=1
    )
    row_payload = payload
    payload = lax.all_to_all(row_payload, DP, 0, 0)
    grad_silu = payload[:, 0, :16].reshape(1, width)
    _, silu_back = jax.vjp(jax.nn.silu, conditioning.astype(F32))
    grad_conditioning = silu_back(grad_silu)[0].astype(BF16)
    out_bias_sum, project_bias_sum, hidden_bias_sum, attend_bias_sum = call(
        bias_kernel,
        (
            shaped((1, 1024), F32),
            shaped((1, 1024), F32),
            shaped((1, 2048), F32),
            shaped((1, 2, 512), F32),
        ),
        (payload[:, 1],),
        10**5,
        core=(place.t.reshape(1).astype(jnp.int32),),
    )

    sent_two = send_plane(blocks_two, False)
    flips = ((0, 0), (0, 1), (1, 0), (1, 1))
    attend_own, forward_own, *attend_rest = call(
        last_sums_kernel,
        (shaped((32, 1024), F32), shaped((2, 16, 2048), F32), shaped((32, 1024)),
         shaped((96, 1024)), shaped((32, 1024))),
        tuple(by_step(blocks_two[0], sent_two)),
        10**6,
        far=(row_payload, grad_ada, ada_bias_sum),
    )
    gate_second = after(mods[5:6], attend_own)
    block_low = (middle + gate_second * branch).astype(BF16)
    moved = swap_layout(jnp.stack([block_low, grad_stream.astype(BF16)]))
    block_output, grad_latents = moved[:1], moved[1:]
    flipped_t, flipped_w, flipped_both = (
        flip_x(item, w, t) for item, (w, t) in zip(attend_rest, flips[1:])
    )
    forward_other = flipped_w[32:].reshape(2, 2, 16, 1024).transpose(0, 2, 1, 3)
    forward_grads = forward_own + forward_other.reshape(2, 16, 2048).astype(F32)
    reduced = add_up(attend_own, [flipped_t, flipped_w[:32], flipped_both]).reshape(2, 16, 1024)
    mine = lax.dynamic_index_in_dim(reduced, place.c, 0, keepdims=False)
    theirs = swap_core(lax.dynamic_index_in_dim(reduced, 1 - place.c, 0, keepdims=False))
    low = jnp.where(place.first, mine, theirs).reshape(16, 4, 256)
    high = jnp.where(place.first, theirs, mine).reshape(16, 4, 256)
    reduced = jnp.concatenate([low, high], axis=2)


    return (
        block_output,
        grad_latents,
        grad_conditioning,
        grad_ada,
        ada_bias_sum,
        reduced[None, :, :3],
        attend_bias_sum,
        reduced[None, :, 3],
        project_bias_sum,
        forward_grads[0][None],
        hidden_bias_sum,
        forward_grads[1][None],
        out_bias_sum,
    )


def solution(mesh):
    fine = Mesh(mesh.devices.reshape(4, 2, 4, 2, 2), ("z", "w", "y", "c", "t"))
    return jax.shard_map(
        shards,
        mesh=fine,
        in_specs=(
            P(DP, "t", None),
            P(DP, None),
            P(DP, "t", None),
            P(DP, None, None),
            P(),
            P(None, DP, None, "t"),
            P(None, None, "t"),
            P(None, DP, "t"),
            P(),
            P(None, DP, "t"),
            P(None, "t"),
            P(None, DP, "t"),
            P(),
        ),
        out_specs=(
            P(DP, "t", None),
            P(DP, "t", None),
            P(DP, None),
            P(DP, None, None),
            P(),
            P(None, DP, None, "t"),
            P(None, None, "t"),
            P(None, DP, "t"),
            P(),
            P(None, DP, "t"),
            P(None, "t"),
            P(None, DP, "t"),
            P(),
        ),
        check_vma=False,
    )
```

```python
import functools
import math

import jax
import jax.numpy as jnp
from jax import lax
from jax.experimental import pallas as pl
from jax.experimental.pallas import tpu as pltpu
from jax.sharding import Mesh
from jax.sharding import PartitionSpec as P

HEAD_DIM = 64
EPS = 1e-06
F32 = jnp.float32
BF16 = jnp.bfloat16
DP = ("z", "w", "y", "c")
CHIPS = ("z", "w", "y", "t")


def normalize(values):
    centered = values - jnp.mean(values, axis=-1, keepdims=True)
    inverse = lax.rsqrt(jnp.mean(centered * centered, axis=-1, keepdims=True) + EPS)
    return (centered * inverse, inverse)


def normalize_back(grad, normed, inverse):
    return inverse * (
        grad
        - jnp.mean(grad, axis=-1, keepdims=True)
        - normed * jnp.mean(grad * normed, axis=-1, keepdims=True)
    )


def dot(left, right):
    return jnp.dot(left, right, preferred_element_type=F32)


def dot_nt(left, right):
    return lax.dot_general(left, right, (((1,), (1,)), ((), ())), preferred_element_type=F32)


def dot_tn(left, right):
    return lax.dot_general(left, right, (((0,), (0,)), ((), ())), preferred_element_type=F32)


def swap_core(piece):
    return lax.ppermute(piece, "c", [(0, 1), (1, 0)])


def swap_t(piece):
    return lax.ppermute(piece, "t", [(0, 1), (1, 0)])


def swap_layout(piece):
    return lax.ppermute(piece, ("c", "t"), [(0, 0), (1, 2), (2, 1), (3, 3)])


def flip_plane(piece, step, last):
    perm = []
    for z in range(4):
        for y in range(4):
            for c in range(2):
                along_z = (c == 0) == last
                z2, y2 = (z ^ step, y) if along_z else (z, y ^ step)
                perm.append(((z * 4 + y) * 2 + c, (z2 * 4 + y2) * 2 + c))
    return lax.ppermute(piece, ("z", "y", "c"), perm)


def flip_x(piece, w_step, t_step):
    perm = [(w * 2 + t, (w ^ w_step) * 2 + (t ^ t_step)) for w in range(2) for t in range(2)]
    return lax.ppermute(piece, ("w", "t"), perm)


STEPS = (2, 1, 3)


def after(value, *others):
    def copy(source, *rest):
        rest[-1][...] = source[...]

    whole = pl.BlockSpec(memory_space=pltpu.VMEM)
    left = pl.BlockSpec(memory_space=pl.ANY)
    return pl.pallas_call(
        copy,
        out_shape=jax.ShapeDtypeStruct(value.shape, value.dtype),
        in_specs=[whole] + [left] * len(others),
        out_specs=whole,
    )(value, *others)


def by_step(own, received):
    return [own] + [received[k] for k in (1, 2, 3)]


def one_hot(order):
    features = lax.broadcasted_iota(jnp.int32, (1024, 1024), 0)
    return (features == order[None, :]).astype(BF16)


class Place:
    def __init__(self):
        self.z = lax.axis_index("z")
        self.w = lax.axis_index("w")
        self.y = lax.axis_index("y")
        self.c = lax.axis_index("c")
        self.t = lax.axis_index("t")
        self.first = self.c == 0

    def attention_order(self):
        place = lax.iota(jnp.int32, 1024)
        last, before, w_step, row = place // 256, place // 64 % 4, place // 32 % 2, place % 32
        z = self.z ^ jnp.where(self.first, last, before)
        y = self.y ^ jnp.where(self.first, before, last)
        return ((z * 2 + (self.w ^ w_step)) * 4 + y) * 32 + row

    def forward_order(self):
        place = lax.iota(jnp.int32, 1024)
        core = self.c ^ (place // 512)
        last, before, w_step, row = place // 128 % 4, place // 32 % 4, place // 16 % 2, place % 16
        z = self.z ^ jnp.where(core == 0, last, before)
        y = self.y ^ jnp.where(core == 0, before, last)
        return ((z * 2 + (self.w ^ w_step)) * 4 + y) * 32 + core * 16 + row


def add_up(own, received):
    total = own.astype(F32)
    for block in received:
        total = total + block.astype(F32)
    return total


def send_plane(blocks, last):
    return {k: flip_plane(blocks[k], k, last) for k in STEPS}


def reduce_plane(blocks, last):
    return add_up(blocks[0], send_plane(blocks, last).values())


TOKENS = 256
WIDTH = 1024
BLOCK = 256
ALL_HEADS = [(t, h) for t in range(2) for h in range(4)]
SCALE = HEAD_DIM ** (-0.5)


def head_columns(t, h):
    return slice(t * 256 + h * HEAD_DIM, t * 256 + (h + 1) * HEAD_DIM)


def weight_rows(block, t, columns):
    rows = [block[k // 2, (k % 2) * 128 + t * 64 : (k % 2) * 128 + (t + 1) * 64, columns] for k in range(4)]
    return jnp.concatenate(rows)


TRIPLE, PROJECT = slice(0, 768), slice(768, 1024)


def places(kept, kept_probs):
    left, right = pl.ds(0, 512), pl.ds(512, 512)
    return (
        kept.at[0],
        kept.at[1, :, left],
        kept.at[1, :, right],
        kept.at[2, :, left],
        kept_probs.at[pl.ds(0, 8)],
        kept.at[2, :, right],
        *(kept.at[pl.ds(4 + 2 * k, 2)] for k in range(4)),
    )


def forward_kernel(
    first, order, w0, w1, w2, w3, bias, one,
    kept, kept_probs, out, rel, query, key, value, probs, mixed, sent,
):
    blocks = (w0, w1, w2, w3)
    copies = [
        pltpu.make_async_copy(source, target, sent.at[i])
        for i, (source, target) in enumerate(
            zip((rel, query, key, value, probs, mixed, *blocks), places(kept, kept_probs))
        )
    ]
    for copy in copies[6:]:
        copy.start()
    rel[...] = dot(first[...], order[...]).astype(BF16)
    copies[0].start()
    for t in range(2):
        packed = sum(
            dot(rel[:, k * BLOCK : (k + 1) * BLOCK], weight_rows(blocks[k], t, TRIPLE))
            for k in range(4)
        )
        columns = slice(t * 256, (t + 1) * 256)
        query[:, columns] = (packed[:, :256] + bias[0:1, columns]).astype(BF16)
        key[:, columns] = packed[:, 256:512].astype(BF16)
        value[:, columns] = (packed[:, 512:768] + bias[1:2, columns]).astype(BF16)
    for copy in copies[1:4]:
        copy.start()
    for t, h in ALL_HEADS:
        columns = head_columns(t, h)
        scores = dot_nt(query[:, columns], key[:, columns]) * SCALE
        expd = jnp.exp(scores - jnp.max(scores, axis=-1, keepdims=True))
        prob = expd / jnp.sum(expd, axis=-1, keepdims=True)
        probs[t * 4 + h] = prob
        mixed[:, columns] = dot(prob.astype(BF16), value[:, columns]).astype(BF16)
    for copy in copies[4:6]:
        copy.start()
    partial = [
        sum(
            dot_nt(mixed[:, t * 256 : (t + 1) * 256], weight_rows(blocks[k], t, PROJECT))
            for t in range(2)
        ).astype(BF16)
        for k in range(4)
    ]
    out[...] = dot_nt(jnp.concatenate(partial, axis=1), order[...]).astype(BF16)
    for copy in copies:
        copy.wait()


def backward_kernel(
    projected, order, kept, kept_probs, one, g0, g1, g2, g3, out, bias,
    packed, back, ready, w0, w1, w2, w3, rel, query, key, value, probs, mixed, sent, arrived,
):
    blocks = (w0, w1, w2, w3)
    fetched = [
        pltpu.make_async_copy(source, target, arrived.at[i])
        for i, (source, target) in enumerate(
            zip(
                places(kept, kept_probs),
                (rel, query, key, value, probs, mixed, w0, w1, w2, w3),
            )
        )
    ]
    for copy in fetched:
        copy.start()
    copies = [
        pltpu.make_async_copy(ready.at[k], target, sent.at[k])
        for k, target in enumerate((g0, g1, g2, g3))
    ]
    back[...] = dot(projected[...], order[...]).astype(BF16)
    for copy in fetched:
        copy.wait()
    for t in range(2):
        grad_mixed = sum(
            dot(back[:, k * BLOCK : (k + 1) * BLOCK], weight_rows(blocks[k], t, PROJECT))
            for k in range(4)
        ).astype(BF16)
        for h in range(4):
            columns = head_columns(t, h)
            grad_head = grad_mixed[:, h * HEAD_DIM : (h + 1) * HEAD_DIM]
            prob = probs[t * 4 + h]
            grad_value = dot_tn(prob.astype(BF16), grad_head)
            grad_probs = dot_nt(grad_head, value[:, columns])
            grad_scores = (
                prob * (grad_probs - jnp.sum(grad_probs * prob, axis=-1, keepdims=True))
            ).astype(BF16)
            grad_query = dot(grad_scores, key[:, columns]) * SCALE
            grad_key = dot_tn(grad_scores, query[:, columns]) * SCALE
            for i, item in enumerate((grad_query, grad_key, grad_value)):
                begin = i * 256 + h * HEAD_DIM
                packed[t, :, begin : begin + HEAD_DIM] = item.astype(BF16)
        for row, begin in enumerate((0, 512)):
            bias[t * 2 + row : t * 2 + row + 1, :] = jnp.sum(
                packed[t, :, begin : begin + 256].astype(F32), axis=0, keepdims=True
            )
    partial = []
    for k in range(4):
        rows = slice(k * BLOCK, (k + 1) * BLOCK)
        for t in range(2):
            ready[k, :, t * 1024 : t * 1024 + 768] = dot_tn(rel[:, rows], packed[t]).astype(BF16)
            ready[k, :, t * 1024 + 768 : (t + 1) * 1024] = dot_tn(
                back[:, rows], mixed[:, t * 256 : (t + 1) * 256]
            ).astype(BF16)
        copies[k].start()
        partial.append(
            sum(dot_nt(packed[t], weight_rows(blocks[k], t, TRIPLE)) for t in range(2)).astype(BF16)
        )
    out[...] = dot_nt(jnp.concatenate(partial, axis=1), order[...]).astype(BF16)
    for copy in copies:
        copy.wait()


def middle_kernel(
    second, branch, order, hidden, m0, m1, m2, m3, t0, t1, t2, t3,
    rel, active, out, back, hidden_sum, mine, theirs, arrived,
):
    copies = []
    for which in range(2):
        for half in range(2):
            for target, blocks in ((mine, (m0, m1, m2, m3)), (theirs, (t0, t1, t2, t3))):
                for k, block in enumerate(blocks):
                    copies.append(
                        pltpu.make_async_copy(
                            block.at[:, :, which * 2 + half],
                            target.at[which, k, :, :, :, pl.ds(half * 1024, 1024)],
                            arrived.at[len(copies)],
                        )
                    )
    for copy in copies:
        copy.start()
    rel[0] = dot(second[...], order[...]).astype(BF16)
    rel[1] = dot(branch[...], order[...]).astype(BF16)
    for copy in copies:
        copy.wait()

    def rows(source, which, columns):
        return source[which, :, :, :, :, columns].reshape(512, columns.stop - columns.start)

    root = (2.0 / math.pi) ** 0.5
    for begin in range(0, 2048, 512):
        columns = slice(begin, begin + 512)
        pre = (
            dot(rel[0, :, :512], rows(mine, 0, columns))
            + dot(rel[0, :, 512:], rows(theirs, 0, columns))
            + hidden[0:1, columns]
        )
        grad_active = dot(rel[1, :, :512], rows(mine, 1, columns)) + dot(
            rel[1, :, 512:], rows(theirs, 1, columns)
        )
        square = pre * pre
        bent = jnp.tanh(root * (pre + 0.044715 * (square * pre)))
        half = 0.5 * (1.0 + bent)
        active[1, :, columns] = (pre * half).astype(BF16)
        slope = half + (0.5 * pre) * (1.0 - bent * bent) * (root * (1.0 + 0.134145 * square))
        low = (grad_active * slope).astype(BF16)
        active[0, :, columns] = low
        hidden_sum[0:1, columns] = jnp.sum(low.astype(F32), axis=0, keepdims=True)
    for which, target in ((0, back), (1, out)):
        partial = jnp.concatenate(
            [
                dot_nt(active[which], rows(item, which, slice(0, 2048))).astype(BF16)
                for item in (mine, theirs)
            ],
            axis=1,
        )
        target[...] = dot_nt(partial, order[...]).astype(BF16)


def rows_kernel(rel, columns, theirs, *outs):
    for k, out in enumerate(outs):
        rows = slice(k * 128, (k + 1) * 128)
        for which in range(2):
            out[which] = (
                dot_tn(rel[which, :, rows], columns[which]) + theirs[which, rows].astype(F32)
            ).astype(BF16)


def total_of(blocks, *index):
    return sum(block[index].astype(F32) for block in blocks)


def join_sums_kernel(*refs):
    attend, forward, outs = refs[:4], refs[4:8], refs[-4:]
    for k, out in enumerate(outs):
        out[0:64] = total_of(attend, slice(k * 64, (k + 1) * 64)).astype(BF16)
        for which in range(2):
            rows = slice(k * 32, (k + 1) * 32)
            out[64 + which * 32 : 96 + which * 32] = total_of(forward, which, rows).astype(BF16)


def last_sums_kernel(b0, b1, b2, b3, one, two, three, attend_own, forward_own, for_t, for_w, for_both):
    blocks = (b0, b1, b2, b3)
    low, high = slice(0, 1024), slice(1024, 2048)
    attend_own[...] = total_of(blocks, slice(0, 32), low)
    for_t[...] = total_of(blocks, slice(0, 32), high).astype(BF16)
    for_w[0:32] = total_of(blocks, slice(32, 64), low).astype(BF16)
    for_both[...] = total_of(blocks, slice(32, 64), high).astype(BF16)
    for which in range(2):
        begin = 64 + which * 32
        forward_own[which] = total_of(blocks, slice(begin, begin + 16))
        for half, columns in enumerate((low, high)):
            at = 32 + (which * 2 + half) * 16
            for_w[at : at + 16] = total_of(blocks, slice(begin + 16, begin + 32), columns).astype(
                BF16
            )


def split_kernel(core, attend, project, hidden, output, mine, theirs, forward, held, arrived):
    copies = [pltpu.make_async_copy(project, held, arrived.at[4])]
    for which, source in enumerate((hidden, output)):
        for half in range(2):
            piece = which * 2 + half
            copies.append(
                pltpu.make_async_copy(
                    source.at[:, pl.ds(half * 1024, 1024)],
                    forward.at[pl.ds(piece * 16, 16)],
                    arrived.at[piece],
                )
            )
    for copy in copies:
        copy.start()
    first = core[0] == 0

    def split(j, rows):
        low, high = rows[:, :256], rows[:, 256:]
        mine[:, j * 256 : (j + 1) * 256] = jnp.where(first, low, high)
        theirs[:, j * 256 : (j + 1) * 256] = jnp.where(first, high, low)

    for j in range(3):
        split(j, attend[:, j, :])
    for copy in copies:
        copy.wait()
    split(3, held[...])


def join_kernel(core, mine, theirs, forward, bias, piece, for_t, for_w):
    first = core[0] == 0
    for target in (piece, for_t, for_w):
        target[0:16] = jnp.where(first, mine[...], theirs[...])
        target[16:32] = jnp.where(first, theirs[...], mine[...])
    for_t[32:48] = bias[...]
    for_w[32:96] = forward[...]


def bias_kernel(t, sums, out, project, hidden, attend):
    on_first = t[0] == 0

    def chunk(j, core):
        return sums[j * 2 + core, 1:2]

    for core in range(2):
        for i in range(4):
            columns = slice(core * 512 + i * 128, core * 512 + (i + 1) * 128)
            out[:, columns] = chunk(i, core)
            project[:, columns] = chunk(4 + i, core)
        for i in range(8):
            columns = slice(core * 1024 + i * 128, core * 1024 + (i + 1) * 128)
            hidden[:, columns] = jnp.where(on_first, chunk(8 + i, core), chunk(16 + i, core))
        for i in range(4):
            begin = core * 256 + i % 2 * 128
            attend[0, i // 2 : i // 2 + 1, begin : begin + 128] = jnp.where(
                on_first, chunk(24 + i, core), chunk(28 + i, core)
            )


def part_kernel(source, one, mods, biases):
    mods[...] = source[:, 0:24]
    biases[...] = source[:, 24].astype(F32)


def pack_kernel(plan, *refs):
    outs = refs[len(refs) - len(plan) :]
    for out, parts in zip(outs, plan):
        at = 0
        for source, begin, rows in parts:
            out[at : at + rows] = refs[source][begin : begin + rows]
            at += rows


def shaped(shape, kind=BF16):
    return jax.ShapeDtypeStruct(shape, kind)


def call(kernel, outs, args, flops, scratch=(), far=(), out_far=0, core=(), limit=12):
    whole = pl.BlockSpec(memory_space=pltpu.VMEM)
    left = pl.BlockSpec(memory_space=pl.ANY)
    moved = sum(item.size * item.dtype.itemsize for item in (*args, *outs))
    return pl.pallas_call(
        kernel,
        out_shape=outs,
        in_specs=[pl.BlockSpec(memory_space=pltpu.SMEM)] * len(core)
        + [whole] * len(args)
        + [left] * len(far),
        out_specs=[left] * out_far + [whole] * (len(outs) - out_far),
        scratch_shapes=list(scratch),
        compiler_params=pltpu.CompilerParams(vmem_limit_bytes=limit * 2**20),
        cost_estimate=pl.CostEstimate(flops=flops, bytes_accessed=moved, transcendentals=0),
    )(*core, *args, *far)


def scratch_like(outs):
    return [pltpu.VMEM(item.shape, item.dtype) for item in outs]


HALF = shaped((256, 512))
KEPT = (shaped((72, 256, 1024)), shaped((144, 256, 256), F32))
SAVED = (shaped((256, 1024)), HALF, HALF, HALF, shaped((8, 256, 256), F32), HALF)


def attention_forward(first, order, blocks, bias, earlier):
    outs = KEPT + (shaped((TOKENS, WIDTH)),)
    scratch = scratch_like(SAVED) + [pltpu.SemaphoreType.DMA((10,))]
    args = (first, order, *blocks, bias)
    return call(forward_kernel, outs, args, 4 * 10**9, scratch, (earlier,), 2, limit=22)


def attention_backward(projected, order, saved, earlier):
    outs = (shaped((BLOCK, 2048)),) * 4 + (shaped((TOKENS, WIDTH)), shaped((4, 256), F32))
    scratch = [
        pltpu.VMEM((2, TOKENS, 768), BF16),
        pltpu.VMEM((TOKENS, WIDTH), BF16),
        pltpu.VMEM((4, BLOCK, 2048), BF16),
        *scratch_like((shaped((2, 256, WIDTH)),) * 4 + SAVED),
        pltpu.SemaphoreType.DMA((4,)),
        pltpu.SemaphoreType.DMA((10,)),
    ]
    return call(backward_kernel, outs, (projected, order), 4 * 10**9, scratch, (*saved, earlier), 4, limit=24)


def feed_forward(second, branch, order, hidden, mine, theirs):
    wide, narrow = shaped((2, TOKENS, 2048)), shaped((TOKENS, WIDTH))
    outs = (shaped((2, TOKENS, WIDTH)), wide, narrow, narrow, shaped((1, 2048), F32))
    scratch = (
        pltpu.VMEM((2, 4, 4, 2, 16, 2048), BF16),
        pltpu.VMEM((2, 4, 4, 2, 16, 2048), BF16),
        pltpu.SemaphoreType.DMA((32,)),
    )
    args = (second, branch, order, hidden)
    return call(middle_kernel, outs, args, 6 * 10**9, scratch, (*mine, *theirs), limit=24)


def pack(inputs, plan, earlier=()):
    outs = tuple(
        shaped((sum(rows for _, _, rows in parts),) + inputs[0].shape[1:]) for parts in plan
    )
    return call(functools.partial(pack_kernel, plan), outs, tuple(inputs), 10**5, far=earlier)


def feed_forward_rows(rel, columns, theirs):
    return call(rows_kernel, (shaped((2, 128, 2048)),) * 4, (rel, columns, theirs), 10**9, limit=20)


def halves(rows):
    half = rows.shape[0] // 2
    return rows[:half], rows[half:]


def shards(
    latents,
    conditioning,
    cotangent,
    modulate_weight,
    modulate_bias,
    attend_weight,
    attend_bias,
    project_weight,
    project_bias,
    hidden_weight,
    hidden_bias,
    output_weight,
    output_bias,
):
    place = Place()
    width = conditioning.shape[1]

    modulate = modulate_weight[:, 0]
    order_a = one_hot(place.attention_order())
    order_f = one_hot(place.forward_order())

    bias_own = lax.dynamic_slice_in_dim(attend_bias[0], place.c * 256, 256, 1)
    bias_rows = jnp.pad(bias_own.reshape(1, 512), ((0, 15), (0, 512)))
    core = place.c.reshape(1).astype(jnp.int32)
    quarter = shaped((16, 1024))
    mine, theirs, forward_piece = call(
        split_kernel,
        (quarter, quarter, shaped((64, 1024))),
        (attend_weight[0],),
        10**5,
        (pltpu.VMEM((16, 512), BF16), pltpu.SemaphoreType.DMA((5,))),
        (project_weight[0], hidden_weight[0], output_weight[0]),
        core=(core,),
    )
    piece, for_t, for_w = call(
        join_kernel,
        (shaped((32, 1024)), shaped((48, 1024)), shaped((96, 1024))),
        (mine, swap_core(theirs), forward_piece, bias_rows),
        10**5,
        core=(core,),
    )
    flipped_w = flip_x(for_w, 1, 0)
    flipped_t = flip_x(for_t, 0, 1)
    flipped_both = flip_x(piece, 1, 1)
    bias_pair = jnp.concatenate([bias_own, flipped_t[32, :512].reshape(2, 256)], axis=1).astype(F32)
    on_first = place.t == 0
    (stage_one,) = pack(
        [piece, flipped_w, flipped_t, flipped_both, forward_piece],
        [[(0, 0, 32), (1, 0, 32), (2, 0, 32), (3, 0, 32), (4, 0, 64), (1, 32, 64)]],
    )

    (moved,) = pack([latents[0], cotangent[0]], [[(0, 0, 128), (1, 0, 128)]], (stage_one,))
    moved = swap_layout(moved)
    stream, grad = moved[:128].astype(F32), moved[128:].astype(F32)

    stage_two = by_step(stage_one, {k: flip_plane(stage_one, k, False) for k in STEPS})
    attend_two, forward_two = pack(
        stage_two, [[(k, begin, 128) for k in range(4)] for begin in (0, 128)]
    )
    attend_got = [flip_plane(attend_two, k, True) for k in (1, 2, 3)]
    attend_blocks = [attend_two] + attend_got
    attend_blocks = [item.reshape(2, 256, WIDTH) for item in attend_blocks]
    forward_got = {k: flip_plane(forward_two, k, True) for k in STEPS}

    silu_rows = lax.all_to_all(
        after(conditioning, piece).reshape(64, 16), DP, 0, 0, tiled=True
    )
    silu_rows = after(silu_rows, attend_two, moved)
    silu_rows = jax.nn.silu(silu_rows.astype(F32)).astype(BF16)

    silu_chip = lax.dynamic_index_in_dim(silu_rows.reshape(32, 2, 16), place.t, 1, keepdims=False)
    terms = dot(silu_chip, modulate).reshape(64, 24, 128)
    terms = lax.all_to_all(terms, DP, 0, 0)
    mods_half = jnp.sum(terms, axis=0).reshape(3072)
    bias_row = after(modulate_bias, attend_got[1])[0].astype(F32)
    mods = lax.all_gather(mods_half, "c", axis=0, tiled=True) + bias_row
    mods = mods.reshape(6, width)

    normed_first, inverse_first = normalize(stream)
    first_in = (normed_first * (1.0 + mods[1]) + mods[0]).astype(BF16)
    first_all = jnp.concatenate([first_in, swap_core(first_in)])
    grad_branch = (grad * mods[5]).astype(BF16)
    out_bias_part = jnp.sum(grad_branch.astype(F32), axis=0)
    branch_other = swap_t(grad_branch)
    branch_all = jnp.concatenate([grad_branch, branch_other])
    *saved, partial = attention_forward(
        first_all, order_a, attend_blocks, bias_pair, forward_got[2]
    )
    own, other = halves(partial)
    projected = (
        own.astype(F32)
        + swap_core(other).astype(F32)
        + after(project_bias, forward_got[1], branch_other).astype(F32)
    )
    middle = stream + mods[2] * projected

    normed_second, inverse_second = normalize(middle)
    second_in = (normed_second * (1.0 + mods[4]) + mods[3]).astype(BF16)
    second_all = jnp.concatenate([second_in, swap_t(second_in)])
    forward_mine = [
        item.reshape(4, 2, 4, 16, 1024) for item in by_step(forward_two, forward_got)
    ]
    forward_theirs = [swap_core(item) for item in forward_mine]
    rel_pair, grad_pair, branch_partial, back_partial, hidden_bias_part = feed_forward(
        second_all, branch_all, order_f, hidden_bias.astype(F32), forward_mine, forward_theirs
    )

    def weight_grads(rows):
        return lax.dot_general(
            rows, grad_pair, (((1,), (1,)), ((0,), (0,))), preferred_element_type=F32
        )

    theirs = swap_core(weight_grads(rel_pair[:, :, 512:]).astype(BF16))
    forward_blocks = feed_forward_rows(rel_pair, grad_pair, theirs)
    forward_sent = send_plane(forward_blocks, True)
    own, other = halves(back_partial)
    branch_own, branch_other = halves(branch_partial)
    received = swap_t(jnp.concatenate([other, branch_other]))
    grad_second = own.astype(F32) + received[:128].astype(F32)
    scale_second = after(mods[4:5], *forward_blocks[1:])
    grad_shift_second = jnp.sum(grad_second, axis=0)
    grad_scale_second = jnp.sum(grad_second * normed_second, axis=0)
    grad_middle = grad + normalize_back(
        grad_second * (1.0 + scale_second), normed_second, inverse_second
    )

    grad_gate_first = jnp.sum(grad_middle * projected, axis=0)
    grad_projected = (grad_middle * mods[2]).astype(BF16)
    project_bias_part = jnp.sum(grad_projected.astype(F32), axis=0)
    projected_all = jnp.concatenate([grad_projected, swap_core(grad_projected)])
    *attend_grads, partial, attend_bias_part = attention_backward(
        projected_all,
        order_a,
        saved,
        forward_sent[1],
    )
    attend_sent = send_plane(attend_grads, True)
    branch = branch_own.astype(F32) + received[128:].astype(F32) + output_bias[0].astype(F32)
    block_low = (middle + mods[5] * branch).astype(BF16)
    grad_gate_second = jnp.sum(grad * branch, axis=0)
    own, other = halves(partial)
    grad_first = own.astype(F32) + swap_core(other).astype(F32)
    scale_first = after(mods[1:2], partial, forward_sent[2], forward_sent[3])
    attend_bias_part = attend_bias_part.reshape(2, 2, 256)
    attend_bias_part = jnp.where(on_first, attend_bias_part, attend_bias_part[::-1])
    grad_shift_first = jnp.sum(grad_first, axis=0)
    grad_scale_first = jnp.sum(grad_first * normed_first, axis=0)
    grad_stream = grad_middle + normalize_back(
        grad_first * (1.0 + scale_first), normed_first, inverse_first
    )
    sums = jnp.concatenate(
        [
            jnp.stack([grad_shift_first, grad_scale_first, grad_gate_first]).reshape(2, 1536),
            jnp.stack([grad_shift_second, grad_scale_second, grad_gate_second]).reshape(2, 1536),
        ],
        axis=0,
    ).reshape(2, 3072)
    sums = jnp.concatenate(
        [
            sums,
            out_bias_part.reshape(2, 512),
            project_bias_part.reshape(2, 512),
            hidden_bias_part.reshape(2, 1024),
        ],
        axis=1,
    )
    sums = lax.dynamic_index_in_dim(sums, place.c, 0, keepdims=False) + swap_core(
        lax.dynamic_index_in_dim(sums, 1 - place.c, 0, keepdims=False)
    )
    sums = after(sums.reshape(40, 128), attend_sent[2]).reshape(5120)
    mod_low = sums[:3072].astype(BF16)
    hidden_sum = sums[4096:]
    biases = jnp.concatenate(
        [
            sums[3072:4096],
            jnp.where(on_first, hidden_sum, 0.0),
            jnp.where(on_first, 0.0, hidden_sum),
            attend_bias_part.reshape(1024),
        ]
    ).astype(BF16)
    chunks = jnp.broadcast_to(biases.reshape(32, 1, 128), (32, 2, 128)).reshape(64, 128)
    payload = jnp.concatenate(
        [jnp.broadcast_to(mod_low.reshape(24, 128), (64, 24, 128)), chunks[:, None]], axis=1
    )
    payload = lax.all_to_all(payload, CHIPS, 0, 0)

    blocks_two = call(
        join_sums_kernel,
        (shaped((128, 2048)),) * 4,
        (*by_step(attend_grads[0], attend_sent), *by_step(forward_blocks[0], forward_sent)),
        10**6,
        limit=24,
    )
    mod_mine, bias_rows = call(
        part_kernel,
        (shaped((64, 24, 128)), shaped((64, 128), F32)),
        (payload,),
        10**5,
        far=(blocks_two[0],),
    )
    bias_chunk = jnp.sum(bias_rows, axis=0)
    mod_mine = mod_mine.reshape(64, 3072)
    mod_theirs = swap_core(mod_mine)
    mod_all = jnp.where(
        place.first,
        jnp.concatenate([mod_mine, mod_theirs], axis=1),
        jnp.concatenate([mod_theirs, mod_mine], axis=1),
    )
    grad_ada = dot_tn(silu_rows, mod_all)[:, None]
    ada_bias_sum = jnp.sum(mod_all.astype(F32), axis=0)[None]
    row_parts = dot_nt(mod_all, modulate)
    payload = jnp.stack(
        [jnp.pad(row_parts, ((0, 0), (0, 112))), jnp.broadcast_to(bias_chunk, (64, 128))], axis=1
    )
    row_payload = payload
    payload = lax.all_to_all(row_payload, DP, 0, 0)
    grad_silu = payload[:, 0, :16].reshape(1, width)
    _, silu_back = jax.vjp(jax.nn.silu, conditioning.astype(F32))
    grad_conditioning = silu_back(grad_silu)[0].astype(BF16)
    out_bias_sum, project_bias_sum, hidden_bias_sum, attend_bias_sum = call(
        bias_kernel,
        (
            shaped((1, 1024), F32),
            shaped((1, 1024), F32),
            shaped((1, 2048), F32),
            shaped((1, 2, 512), F32),
        ),
        (payload,),
        10**5,
        core=(place.t.reshape(1).astype(jnp.int32),),
    )

    sent_two = send_plane(blocks_two, False)
    flips = ((0, 0), (0, 1), (1, 0), (1, 1))
    attend_own, forward_own, *attend_rest = call(
        last_sums_kernel,
        (shaped((32, 1024), F32), shaped((2, 16, 2048), F32), shaped((32, 1024)),
         shaped((96, 1024)), shaped((32, 1024))),
        tuple(by_step(blocks_two[0], sent_two)),
        10**6,
        far=(row_payload, grad_ada, ada_bias_sum),
    )
    (moved,) = pack(
        [block_low, grad_stream.astype(BF16)], [[(0, 0, 128), (1, 0, 128)]], (attend_own,)
    )
    moved = swap_layout(moved).reshape(2, 128, 1024)
    block_output, grad_latents = moved[:1], moved[1:]
    flipped_t, flipped_w, flipped_both = (
        flip_x(item, w, t) for item, (w, t) in zip(attend_rest, flips[1:])
    )
    forward_other = flipped_w[32:].reshape(2, 2, 16, 1024).transpose(0, 2, 1, 3)
    forward_grads = forward_own + forward_other.reshape(2, 16, 2048).astype(F32)
    reduced = add_up(attend_own, [flipped_t, flipped_w[:32], flipped_both]).reshape(2, 16, 1024)
    mine = lax.dynamic_index_in_dim(reduced, place.c, 0, keepdims=False)
    theirs = swap_core(lax.dynamic_index_in_dim(reduced, 1 - place.c, 0, keepdims=False))
    low = jnp.where(place.first, mine, theirs).reshape(16, 4, 256)
    high = jnp.where(place.first, theirs, mine).reshape(16, 4, 256)
    reduced = jnp.concatenate([low, high], axis=2)


    return (
        block_output,
        grad_latents,
        grad_conditioning,
        grad_ada,
        ada_bias_sum,
        reduced[None, :, :3],
        attend_bias_sum,
        reduced[None, :, 3],
        project_bias_sum,
        forward_grads[0][None],
        hidden_bias_sum,
        forward_grads[1][None],
        out_bias_sum,
    )


def solution(mesh):
    fine = Mesh(mesh.devices.reshape(4, 2, 4, 2, 2), ("z", "w", "y", "c", "t"))
    return jax.shard_map(
        shards,
        mesh=fine,
        in_specs=(
            P(DP, "t", None),
            P(DP, None),
            P(DP, "t", None),
            P(DP, None, None),
            P(),
            P(None, DP, None, "t"),
            P(None, None, "t"),
            P(None, DP, "t"),
            P(),
            P(None, DP, "t"),
            P(None, "t"),
            P(None, DP, "t"),
            P(),
        ),
        out_specs=(
            P(DP, "t", None),
            P(DP, "t", None),
            P(DP, None),
            P(DP, None, None),
            P(),
            P(None, DP, None, "t"),
            P(None, None, "t"),
            P(None, DP, "t"),
            P(),
            P(None, DP, "t"),
            P(None, "t"),
            P(None, DP, "t"),
            P(),
        ),
        check_vma=False,
    )
```

```python
import functools
import math

import jax
import jax.numpy as jnp
from jax import lax
from jax.experimental import pallas as pl
from jax.experimental.pallas import tpu as pltpu
from jax.sharding import Mesh
from jax.sharding import PartitionSpec as P

HEAD_DIM = 64
EPS = 1e-06
F32 = jnp.float32
BF16 = jnp.bfloat16
DP = ("z", "w", "y", "c")
CHIPS = ("z", "w", "y", "t")


def normalize(values):
    centered = values - jnp.mean(values, axis=-1, keepdims=True)
    inverse = lax.rsqrt(jnp.mean(centered * centered, axis=-1, keepdims=True) + EPS)
    return (centered * inverse, inverse)


def normalize_back(grad, normed, inverse):
    return inverse * (
        grad
        - jnp.mean(grad, axis=-1, keepdims=True)
        - normed * jnp.mean(grad * normed, axis=-1, keepdims=True)
    )


def dot(left, right):
    return jnp.dot(left, right, preferred_element_type=F32)


def dot_nt(left, right):
    return lax.dot_general(left, right, (((1,), (1,)), ((), ())), preferred_element_type=F32)


def dot_tn(left, right):
    return lax.dot_general(left, right, (((0,), (0,)), ((), ())), preferred_element_type=F32)


def swap_core(piece):
    return lax.ppermute(piece, "c", [(0, 1), (1, 0)])


def swap_t(piece):
    return lax.ppermute(piece, "t", [(0, 1), (1, 0)])


def swap_layout(piece):
    return lax.ppermute(piece, ("c", "t"), [(0, 0), (1, 2), (2, 1), (3, 3)])


def flip_plane(piece, step, last):
    perm = []
    for z in range(4):
        for y in range(4):
            for c in range(2):
                along_z = (c == 0) == last
                z2, y2 = (z ^ step, y) if along_z else (z, y ^ step)
                perm.append(((z * 4 + y) * 2 + c, (z2 * 4 + y2) * 2 + c))
    return lax.ppermute(piece, ("z", "y", "c"), perm)


def flip_x(piece, w_step, t_step):
    perm = [(w * 2 + t, (w ^ w_step) * 2 + (t ^ t_step)) for w in range(2) for t in range(2)]
    return lax.ppermute(piece, ("w", "t"), perm)


STEPS = (2, 1, 3)


def after(value, *others):
    def copy(source, *rest):
        rest[-1][...] = source[...]

    whole = pl.BlockSpec(memory_space=pltpu.VMEM)
    left = pl.BlockSpec(memory_space=pl.ANY)
    return pl.pallas_call(
        copy,
        out_shape=jax.ShapeDtypeStruct(value.shape, value.dtype),
        in_specs=[whole] + [left] * len(others),
        out_specs=whole,
    )(value, *others)


def by_step(own, received):
    return [own] + [received[k] for k in (1, 2, 3)]


def one_hot(order):
    features = lax.broadcasted_iota(jnp.int32, (1024, 1024), 0)
    return (features == order[None, :]).astype(BF16)


class Place:
    def __init__(self):
        self.z = lax.axis_index("z")
        self.w = lax.axis_index("w")
        self.y = lax.axis_index("y")
        self.c = lax.axis_index("c")
        self.t = lax.axis_index("t")
        self.first = self.c == 0

    def attention_order(self):
        place = lax.iota(jnp.int32, 1024)
        last, before, w_step, row = place // 256, place // 64 % 4, place // 32 % 2, place % 32
        z = self.z ^ jnp.where(self.first, last, before)
        y = self.y ^ jnp.where(self.first, before, last)
        return ((z * 2 + (self.w ^ w_step)) * 4 + y) * 32 + row

    def forward_order(self):
        place = lax.iota(jnp.int32, 1024)
        core = self.c ^ (place // 512)
        last, before, w_step, row = place // 128 % 4, place // 32 % 4, place // 16 % 2, place % 16
        z = self.z ^ jnp.where(core == 0, last, before)
        y = self.y ^ jnp.where(core == 0, before, last)
        return ((z * 2 + (self.w ^ w_step)) * 4 + y) * 32 + core * 16 + row


def add_up(own, received):
    total = own.astype(F32)
    for block in received:
        total = total + block.astype(F32)
    return total


def send_plane(blocks, last):
    return {k: flip_plane(blocks[k], k, last) for k in STEPS}


def reduce_plane(blocks, last):
    return add_up(blocks[0], send_plane(blocks, last).values())


TOKENS = 256
WIDTH = 1024
BLOCK = 256
ALL_HEADS = [(t, h) for t in range(2) for h in range(4)]
SCALE = HEAD_DIM ** (-0.5)


def head_columns(t, h):
    return slice(t * 256 + h * HEAD_DIM, t * 256 + (h + 1) * HEAD_DIM)


def weight_rows(block, t, columns):
    rows = [block[k // 2, (k % 2) * 128 + t * 64 : (k % 2) * 128 + (t + 1) * 64, columns] for k in range(4)]
    return jnp.concatenate(rows)


TRIPLE, PROJECT = slice(0, 768), slice(768, 1024)


def places(kept, kept_probs):
    left, right = pl.ds(0, 512), pl.ds(512, 512)
    return (
        kept.at[0],
        kept.at[1, :, left],
        kept.at[1, :, right],
        kept.at[2, :, left],
        kept_probs.at[pl.ds(0, 8)],
        kept.at[2, :, right],
        *(kept.at[pl.ds(4 + 2 * k, 2)] for k in range(4)),
    )


def forward_kernel(
    first, order, w0, w1, w2, w3, bias, one,
    kept, kept_probs, out, rel, query, key, value, probs, mixed, sent,
):
    blocks = (w0, w1, w2, w3)
    copies = [
        pltpu.make_async_copy(source, target, sent.at[i])
        for i, (source, target) in enumerate(
            zip((rel, query, key, value, probs, mixed, *blocks), places(kept, kept_probs))
        )
    ]
    for copy in copies[6:]:
        copy.start()
    rel[...] = dot(first[...], order[...]).astype(BF16)
    copies[0].start()
    for t in range(2):
        packed = sum(
            dot(rel[:, k * BLOCK : (k + 1) * BLOCK], weight_rows(blocks[k], t, TRIPLE))
            for k in range(4)
        )
        columns = slice(t * 256, (t + 1) * 256)
        query[:, columns] = (packed[:, :256] + bias[0:1, columns]).astype(BF16)
        key[:, columns] = packed[:, 256:512].astype(BF16)
        value[:, columns] = (packed[:, 512:768] + bias[1:2, columns]).astype(BF16)
    for copy in copies[1:4]:
        copy.start()
    for t, h in ALL_HEADS:
        columns = head_columns(t, h)
        scores = dot_nt(query[:, columns], key[:, columns]) * SCALE
        expd = jnp.exp(scores - jnp.max(scores, axis=-1, keepdims=True))
        prob = expd / jnp.sum(expd, axis=-1, keepdims=True)
        probs[t * 4 + h] = prob
        mixed[:, columns] = dot(prob.astype(BF16), value[:, columns]).astype(BF16)
    for copy in copies[4:6]:
        copy.start()
    partial = [
        sum(
            dot_nt(mixed[:, t * 256 : (t + 1) * 256], weight_rows(blocks[k], t, PROJECT))
            for t in range(2)
        ).astype(BF16)
        for k in range(4)
    ]
    out[...] = dot_nt(jnp.concatenate(partial, axis=1), order[...]).astype(BF16)
    for copy in copies:
        copy.wait()


def backward_kernel(
    projected, order, kept, kept_probs, one, g0, g1, g2, g3, out, bias,
    packed, back, ready, w0, w1, w2, w3, rel, query, key, value, probs, mixed, sent, arrived,
):
    blocks = (w0, w1, w2, w3)
    fetched = [
        pltpu.make_async_copy(source, target, arrived.at[i])
        for i, (source, target) in enumerate(
            zip(
                places(kept, kept_probs),
                (rel, query, key, value, probs, mixed, w0, w1, w2, w3),
            )
        )
    ]
    for copy in fetched:
        copy.start()
    copies = [
        pltpu.make_async_copy(ready.at[k], target, sent.at[k])
        for k, target in enumerate((g0, g1, g2, g3))
    ]
    back[...] = dot(projected[...], order[...]).astype(BF16)
    for copy in fetched:
        copy.wait()
    for t in range(2):
        grad_mixed = sum(
            dot(back[:, k * BLOCK : (k + 1) * BLOCK], weight_rows(blocks[k], t, PROJECT))
            for k in range(4)
        ).astype(BF16)
        for h in range(4):
            columns = head_columns(t, h)
            grad_head = grad_mixed[:, h * HEAD_DIM : (h + 1) * HEAD_DIM]
            prob = probs[t * 4 + h]
            grad_value = dot_tn(prob.astype(BF16), grad_head)
            grad_probs = dot_nt(grad_head, value[:, columns])
            grad_scores = (
                prob * (grad_probs - jnp.sum(grad_probs * prob, axis=-1, keepdims=True))
            ).astype(BF16)
            grad_query = dot(grad_scores, key[:, columns]) * SCALE
            grad_key = dot_tn(grad_scores, query[:, columns]) * SCALE
            for i, item in enumerate((grad_query, grad_key, grad_value)):
                begin = i * 256 + h * HEAD_DIM
                packed[t, :, begin : begin + HEAD_DIM] = item.astype(BF16)
        for row, begin in enumerate((0, 512)):
            bias[t * 2 + row : t * 2 + row + 1, :] = jnp.sum(
                packed[t, :, begin : begin + 256].astype(F32), axis=0, keepdims=True
            )
    partial = []
    for k in range(4):
        rows = slice(k * BLOCK, (k + 1) * BLOCK)
        for t in range(2):
            ready[k, :, t * 1024 : t * 1024 + 768] = dot_tn(rel[:, rows], packed[t]).astype(BF16)
            ready[k, :, t * 1024 + 768 : (t + 1) * 1024] = dot_tn(
                back[:, rows], mixed[:, t * 256 : (t + 1) * 256]
            ).astype(BF16)
        copies[k].start()
        partial.append(
            sum(dot_nt(packed[t], weight_rows(blocks[k], t, TRIPLE)) for t in range(2)).astype(BF16)
        )
    out[...] = dot_nt(jnp.concatenate(partial, axis=1), order[...]).astype(BF16)
    for copy in copies:
        copy.wait()


def middle_kernel(
    second, branch, order, hidden, m0, m1, m2, m3, t0, t1, t2, t3,
    rel, active, out, back, hidden_sum, mine, theirs, arrived,
):
    copies = []
    for which in range(2):
        for half in range(2):
            for target, blocks in ((mine, (m0, m1, m2, m3)), (theirs, (t0, t1, t2, t3))):
                for k, block in enumerate(blocks):
                    copies.append(
                        pltpu.make_async_copy(
                            block.at[:, :, which * 2 + half],
                            target.at[which, k, :, :, :, pl.ds(half * 1024, 1024)],
                            arrived.at[len(copies)],
                        )
                    )
    for copy in copies:
        copy.start()
    rel[0] = dot(second[...], order[...]).astype(BF16)
    rel[1] = dot(branch[...], order[...]).astype(BF16)
    for copy in copies:
        copy.wait()

    def rows(source, which, columns):
        return source[which, :, :, :, :, columns].reshape(512, columns.stop - columns.start)

    root = (2.0 / math.pi) ** 0.5
    for begin in range(0, 2048, 512):
        columns = slice(begin, begin + 512)
        pre = (
            dot(rel[0, :, :512], rows(mine, 0, columns))
            + dot(rel[0, :, 512:], rows(theirs, 0, columns))
            + hidden[0:1, columns]
        )
        grad_active = dot(rel[1, :, :512], rows(mine, 1, columns)) + dot(
            rel[1, :, 512:], rows(theirs, 1, columns)
        )
        square = pre * pre
        bent = jnp.tanh(root * (pre + 0.044715 * (square * pre)))
        half = 0.5 * (1.0 + bent)
        active[1, :, columns] = (pre * half).astype(BF16)
        slope = half + (0.5 * pre) * (1.0 - bent * bent) * (root * (1.0 + 0.134145 * square))
        low = (grad_active * slope).astype(BF16)
        active[0, :, columns] = low
        hidden_sum[0:1, columns] = jnp.sum(low.astype(F32), axis=0, keepdims=True)
    for which, target in ((0, back), (1, out)):
        partial = jnp.concatenate(
            [
                dot_nt(active[which], rows(item, which, slice(0, 2048))).astype(BF16)
                for item in (mine, theirs)
            ],
            axis=1,
        )
        target[...] = dot_nt(partial, order[...]).astype(BF16)


def rows_kernel(rel, columns, theirs, *outs):
    for k, out in enumerate(outs):
        rows = slice(k * 128, (k + 1) * 128)
        for which in range(2):
            out[which] = (
                dot_tn(rel[which, :, rows], columns[which]) + theirs[which, rows].astype(F32)
            ).astype(BF16)


def total_of(blocks, *index):
    return sum(block[index].astype(F32) for block in blocks)


def join_sums_kernel(*refs):
    attend, forward, outs = refs[:4], refs[4:8], refs[-4:]
    for k, out in enumerate(outs):
        out[0:64] = total_of(attend, slice(k * 64, (k + 1) * 64)).astype(BF16)
        for which in range(2):
            rows = slice(k * 32, (k + 1) * 32)
            out[64 + which * 32 : 96 + which * 32] = total_of(forward, which, rows).astype(BF16)


def last_sums_kernel(b0, b1, b2, b3, one, two, three, attend_own, forward_own, for_t, for_w, for_both):
    blocks = (b0, b1, b2, b3)
    low, high = slice(0, 1024), slice(1024, 2048)
    attend_own[...] = total_of(blocks, slice(0, 32), low)
    for_t[...] = total_of(blocks, slice(0, 32), high).astype(BF16)
    for_w[0:32] = total_of(blocks, slice(32, 64), low).astype(BF16)
    for_both[...] = total_of(blocks, slice(32, 64), high).astype(BF16)
    for which in range(2):
        begin = 64 + which * 32
        forward_own[which] = total_of(blocks, slice(begin, begin + 16))
        for half, columns in enumerate((low, high)):
            at = 32 + (which * 2 + half) * 16
            for_w[at : at + 16] = total_of(blocks, slice(begin + 16, begin + 32), columns).astype(
                BF16
            )


def split_kernel(core, attend, project, hidden, output, mine, theirs, forward, held, arrived):
    copies = [pltpu.make_async_copy(project, held, arrived.at[4])]
    for which, source in enumerate((hidden, output)):
        for half in range(2):
            piece = which * 2 + half
            copies.append(
                pltpu.make_async_copy(
                    source.at[:, pl.ds(half * 1024, 1024)],
                    forward.at[pl.ds(piece * 16, 16)],
                    arrived.at[piece],
                )
            )
    for copy in copies:
        copy.start()
    first = core[0] == 0

    def split(j, rows):
        low, high = rows[:, :256], rows[:, 256:]
        mine[:, j * 256 : (j + 1) * 256] = jnp.where(first, low, high)
        theirs[:, j * 256 : (j + 1) * 256] = jnp.where(first, high, low)

    for j in range(3):
        split(j, attend[j])
    for copy in copies:
        copy.wait()
    split(3, held[...])


def join_kernel(core, mine, theirs, forward, bias, piece, for_t, for_w):
    first = core[0] == 0
    for target in (piece, for_t, for_w):
        target[0:16] = jnp.where(first, mine[...], theirs[...])
        target[16:32] = jnp.where(first, theirs[...], mine[...])
    for_t[32:48] = bias[...]
    for_w[32:96] = forward[...]


def bias_kernel(t, sums, out, project, hidden, attend):
    on_first = t[0] == 0

    def chunk(j, core):
        return sums[j * 2 + core, 1:2]

    for core in range(2):
        for i in range(4):
            columns = slice(core * 512 + i * 128, core * 512 + (i + 1) * 128)
            out[:, columns] = chunk(i, core)
            project[:, columns] = chunk(4 + i, core)
        for i in range(8):
            columns = slice(core * 1024 + i * 128, core * 1024 + (i + 1) * 128)
            hidden[:, columns] = jnp.where(on_first, chunk(8 + i, core), chunk(16 + i, core))
        for i in range(4):
            begin = core * 256 + i % 2 * 128
            attend[0, i // 2 : i // 2 + 1, begin : begin + 128] = jnp.where(
                on_first, chunk(24 + i, core), chunk(28 + i, core)
            )


def part_kernel(source, one, mods, biases):
    whole = source[...].astype(F32)
    mods[...] = whole[:, 0:24].astype(BF16)
    biases[...] = whole[:, 24]


def pack_kernel(plan, *refs):
    outs = refs[len(refs) - len(plan) :]
    for out, parts in zip(outs, plan):
        at = 0
        for source, begin, rows in parts:
            out[at : at + rows] = refs[source][begin : begin + rows]
            at += rows


def shaped(shape, kind=BF16):
    return jax.ShapeDtypeStruct(shape, kind)


def call(kernel, outs, args, flops, scratch=(), far=(), out_far=0, core=(), limit=12):
    whole = pl.BlockSpec(memory_space=pltpu.VMEM)
    left = pl.BlockSpec(memory_space=pl.ANY)
    moved = sum(item.size * item.dtype.itemsize for item in (*args, *outs))
    return pl.pallas_call(
        kernel,
        out_shape=outs,
        in_specs=[pl.BlockSpec(memory_space=pltpu.SMEM)] * len(core)
        + [whole] * len(args)
        + [left] * len(far),
        out_specs=[left] * out_far + [whole] * (len(outs) - out_far),
        scratch_shapes=list(scratch),
        compiler_params=pltpu.CompilerParams(vmem_limit_bytes=limit * 2**20),
        cost_estimate=pl.CostEstimate(flops=flops, bytes_accessed=moved, transcendentals=0),
    )(*core, *args, *far)


def scratch_like(outs):
    return [pltpu.VMEM(item.shape, item.dtype) for item in outs]


HALF = shaped((256, 512))
KEPT = (shaped((72, 256, 1024)), shaped((144, 256, 256), F32))
SAVED = (shaped((256, 1024)), HALF, HALF, HALF, shaped((8, 256, 256), F32), HALF)


def attention_forward(first, order, blocks, bias, earlier):
    outs = KEPT + (shaped((TOKENS, WIDTH)),)
    scratch = scratch_like(SAVED) + [pltpu.SemaphoreType.DMA((10,))]
    args = (first, order, *blocks, bias)
    return call(forward_kernel, outs, args, 4 * 10**9, scratch, (earlier,), 2, limit=22)


def attention_backward(projected, order, saved, earlier):
    outs = (shaped((BLOCK, 2048)),) * 4 + (shaped((TOKENS, WIDTH)), shaped((4, 256), F32))
    scratch = [
        pltpu.VMEM((2, TOKENS, 768), BF16),
        pltpu.VMEM((TOKENS, WIDTH), BF16),
        pltpu.VMEM((4, BLOCK, 2048), BF16),
        *scratch_like((shaped((2, 256, WIDTH)),) * 4 + SAVED),
        pltpu.SemaphoreType.DMA((4,)),
        pltpu.SemaphoreType.DMA((10,)),
    ]
    return call(backward_kernel, outs, (projected, order), 4 * 10**9, scratch, (*saved, earlier), 4, limit=24)


def feed_forward(second, branch, order, hidden, mine, theirs):
    wide, narrow = shaped((2, TOKENS, 2048)), shaped((TOKENS, WIDTH))
    outs = (shaped((2, TOKENS, WIDTH)), wide, narrow, narrow, shaped((1, 2048), F32))
    scratch = (
        pltpu.VMEM((2, 4, 4, 2, 16, 2048), BF16),
        pltpu.VMEM((2, 4, 4, 2, 16, 2048), BF16),
        pltpu.SemaphoreType.DMA((32,)),
    )
    args = (second, branch, order, hidden)
    return call(middle_kernel, outs, args, 6 * 10**9, scratch, (*mine, *theirs), limit=24)


def pack(inputs, plan, earlier=()):
    outs = tuple(
        shaped((sum(rows for _, _, rows in parts),) + inputs[0].shape[1:]) for parts in plan
    )
    return call(functools.partial(pack_kernel, plan), outs, tuple(inputs), 10**5, far=earlier)


def feed_forward_rows(rel, columns, theirs):
    return call(rows_kernel, (shaped((2, 128, 2048)),) * 4, (rel, columns, theirs), 10**9, limit=20)


def halves(rows):
    half = rows.shape[0] // 2
    return rows[:half], rows[half:]


def shards(
    latents,
    conditioning,
    cotangent,
    modulate_weight,
    modulate_bias,
    attend_weight,
    attend_bias,
    project_weight,
    project_bias,
    hidden_weight,
    hidden_bias,
    output_weight,
    output_bias,
):
    place = Place()
    width = conditioning.shape[1]

    modulate = modulate_weight[:, 0]
    order_a = one_hot(place.attention_order())
    order_f = one_hot(place.forward_order())

    bias_own = lax.dynamic_slice_in_dim(attend_bias[0], place.c * 256, 256, 1)
    bias_rows = jnp.pad(bias_own.reshape(1, 512), ((0, 15), (0, 512)))
    core = place.c.reshape(1).astype(jnp.int32)
    quarter = shaped((16, 1024))
    mine, theirs, forward_piece = call(
        split_kernel,
        (quarter, quarter, shaped((64, 1024))),
        (attend_weight[0].transpose(1, 0, 2),),
        10**5,
        (pltpu.VMEM((16, 512), BF16), pltpu.SemaphoreType.DMA((5,))),
        (project_weight[0], hidden_weight[0], output_weight[0]),
        core=(core,),
    )
    piece, for_t, for_w = call(
        join_kernel,
        (shaped((32, 1024)), shaped((48, 1024)), shaped((96, 1024))),
        (mine, swap_core(theirs), forward_piece, bias_rows),
        10**5,
        core=(core,),
    )
    flipped_w = flip_x(for_w, 1, 0)
    flipped_t = flip_x(for_t, 0, 1)
    flipped_both = flip_x(piece, 1, 1)
    bias_pair = jnp.concatenate([bias_own, flipped_t[32, :512].reshape(2, 256)], axis=1).astype(F32)
    on_first = place.t == 0
    (stage_one,) = pack(
        [piece, flipped_w, flipped_t, flipped_both, forward_piece],
        [[(0, 0, 32), (1, 0, 32), (2, 0, 32), (3, 0, 32), (4, 0, 64), (1, 32, 64)]],
    )

    (moved,) = pack([latents[0], cotangent[0]], [[(0, 0, 128), (1, 0, 128)]], (stage_one,))
    moved = swap_layout(moved)
    stream, grad = moved[:128].astype(F32), moved[128:].astype(F32)

    stage_two = by_step(stage_one, {k: flip_plane(stage_one, k, False) for k in STEPS})
    attend_two, forward_two = pack(
        stage_two, [[(k, begin, 128) for k in range(4)] for begin in (0, 128)]
    )
    attend_got = [flip_plane(attend_two, k, True) for k in (1, 2, 3)]
    attend_blocks = [attend_two] + attend_got
    attend_blocks = [item.reshape(2, 256, WIDTH) for item in attend_blocks]
    forward_got = {k: flip_plane(forward_two, k, True) for k in STEPS}

    silu_rows = lax.all_to_all(
        after(conditioning, piece).reshape(64, 16), DP, 0, 0, tiled=True
    )
    silu_rows = after(silu_rows, attend_two, moved)
    silu_rows = jax.nn.silu(silu_rows.astype(F32)).astype(BF16)

    silu_chip = lax.dynamic_index_in_dim(silu_rows.reshape(32, 2, 16), place.t, 1, keepdims=False)
    terms = dot(silu_chip, modulate).reshape(64, 24, 128)
    terms = lax.all_to_all(terms, DP, 0, 0)
    mods_half = jnp.sum(terms, axis=0).reshape(3072)
    bias_row = after(modulate_bias, attend_got[1])[0].astype(F32)
    mods = lax.all_gather(mods_half, "c", axis=0, tiled=True) + bias_row
    mods = mods.reshape(6, width)

    normed_first, inverse_first = normalize(stream)
    first_in = (normed_first * (1.0 + mods[1]) + mods[0]).astype(BF16)
    first_all = jnp.concatenate([first_in, swap_core(first_in)])
    grad_branch = (grad * mods[5]).astype(BF16)
    out_bias_part = jnp.sum(grad_branch.astype(F32), axis=0)
    branch_other = swap_t(grad_branch)
    branch_all = jnp.concatenate([grad_branch, branch_other])
    *saved, partial = attention_forward(
        first_all, order_a, attend_blocks, bias_pair, forward_got[2]
    )
    own, other = halves(partial)
    projected = (
        own.astype(F32)
        + swap_core(other).astype(F32)
        + after(project_bias, forward_got[1], branch_other).astype(F32)
    )
    middle = stream + mods[2] * projected

    normed_second, inverse_second = normalize(middle)
    second_in = (normed_second * (1.0 + mods[4]) + mods[3]).astype(BF16)
    second_all = jnp.concatenate([second_in, swap_t(second_in)])
    forward_mine = [
        item.reshape(4, 2, 4, 16, 1024) for item in by_step(forward_two, forward_got)
    ]
    forward_theirs = [swap_core(item) for item in forward_mine]
    rel_pair, grad_pair, branch_partial, back_partial, hidden_bias_part = feed_forward(
        second_all, branch_all, order_f, hidden_bias.astype(F32), forward_mine, forward_theirs
    )

    def weight_grads(rows):
        return lax.dot_general(
            rows, grad_pair, (((1,), (1,)), ((0,), (0,))), preferred_element_type=F32
        )

    theirs = swap_core(weight_grads(rel_pair[:, :, 512:]).astype(BF16))
    forward_blocks = feed_forward_rows(rel_pair, grad_pair, theirs)
    forward_sent = send_plane(forward_blocks, True)
    own, other = halves(back_partial)
    branch_own, branch_other = halves(branch_partial)
    received = swap_t(jnp.concatenate([other, branch_other]))
    grad_second = own.astype(F32) + received[:128].astype(F32)
    scale_second = after(mods[4:5], *forward_blocks[1:])
    grad_shift_second = jnp.sum(grad_second, axis=0)
    grad_scale_second = jnp.sum(grad_second * normed_second, axis=0)
    grad_middle = grad + normalize_back(
        grad_second * (1.0 + scale_second), normed_second, inverse_second
    )

    grad_gate_first = jnp.sum(grad_middle * projected, axis=0)
    grad_projected = (grad_middle * mods[2]).astype(BF16)
    project_bias_part = jnp.sum(grad_projected.astype(F32), axis=0)
    projected_all = jnp.concatenate([grad_projected, swap_core(grad_projected)])
    *attend_grads, partial, attend_bias_part = attention_backward(
        projected_all,
        order_a,
        saved,
        forward_sent[1],
    )
    attend_sent = send_plane(attend_grads, True)
    branch = branch_own.astype(F32) + received[128:].astype(F32) + output_bias[0].astype(F32)
    block_low = (middle + mods[5] * branch).astype(BF16)
    grad_gate_second = jnp.sum(grad * branch, axis=0)
    own, other = halves(partial)
    grad_first = own.astype(F32) + swap_core(other).astype(F32)
    scale_first = after(mods[1:2], partial, forward_sent[2], forward_sent[3])
    attend_bias_part = attend_bias_part.reshape(2, 2, 256)
    attend_bias_part = jnp.where(on_first, attend_bias_part, attend_bias_part[::-1])
    grad_shift_first = jnp.sum(grad_first, axis=0)
    grad_scale_first = jnp.sum(grad_first * normed_first, axis=0)
    grad_stream = grad_middle + normalize_back(
        grad_first * (1.0 + scale_first), normed_first, inverse_first
    )
    sums = jnp.concatenate(
        [
            jnp.stack([grad_shift_first, grad_scale_first, grad_gate_first]).reshape(2, 1536),
            jnp.stack([grad_shift_second, grad_scale_second, grad_gate_second]).reshape(2, 1536),
        ],
        axis=0,
    ).reshape(2, 3072)
    sums = jnp.concatenate(
        [
            sums,
            out_bias_part.reshape(2, 512),
            project_bias_part.reshape(2, 512),
            hidden_bias_part.reshape(2, 1024),
        ],
        axis=1,
    )
    sums = lax.dynamic_index_in_dim(sums, place.c, 0, keepdims=False) + swap_core(
        lax.dynamic_index_in_dim(sums, 1 - place.c, 0, keepdims=False)
    )
    sums = after(sums.reshape(40, 128), attend_sent[2]).reshape(5120)
    mod_low = sums[:3072].astype(BF16)
    hidden_sum = sums[4096:]
    biases = jnp.concatenate(
        [
            sums[3072:4096],
            jnp.where(on_first, hidden_sum, 0.0),
            jnp.where(on_first, 0.0, hidden_sum),
            attend_bias_part.reshape(1024),
        ]
    ).astype(BF16)
    chunks = jnp.broadcast_to(biases.reshape(32, 1, 128), (32, 2, 128)).reshape(64, 128)
    payload = jnp.concatenate(
        [jnp.broadcast_to(mod_low.reshape(24, 128), (64, 24, 128)), chunks[:, None]], axis=1
    )
    payload = lax.all_to_all(payload, CHIPS, 0, 0)

    blocks_two = call(
        join_sums_kernel,
        (shaped((128, 2048)),) * 4,
        (*by_step(attend_grads[0], attend_sent), *by_step(forward_blocks[0], forward_sent)),
        10**6,
        limit=24,
    )
    mod_mine, bias_rows = call(
        part_kernel,
        (shaped((64, 24, 128)), shaped((64, 128), F32)),
        (payload,),
        10**5,
        far=(blocks_two[0],),
    )
    bias_chunk = jnp.sum(bias_rows, axis=0)
    mod_mine = mod_mine.reshape(64, 3072)
    mod_theirs = swap_core(mod_mine)
    mod_all = jnp.where(
        place.first,
        jnp.concatenate([mod_mine, mod_theirs], axis=1),
        jnp.concatenate([mod_theirs, mod_mine], axis=1),
    )
    grad_ada = dot_tn(silu_rows, mod_all)[:, None]
    ada_bias_sum = jnp.sum(mod_all.astype(F32), axis=0)[None]
    row_parts = dot_nt(mod_all, modulate)
    payload = jnp.stack(
        [jnp.pad(row_parts, ((0, 0), (0, 112))), jnp.broadcast_to(bias_chunk, (64, 128))], axis=1
    )
    row_payload = payload
    payload = lax.all_to_all(row_payload, DP, 0, 0)
    grad_silu = payload[:, 0, :16].reshape(1, width)
    _, silu_back = jax.vjp(jax.nn.silu, conditioning.astype(F32))
    grad_conditioning = silu_back(grad_silu)[0].astype(BF16)
    out_bias_sum, project_bias_sum, hidden_bias_sum, attend_bias_sum = call(
        bias_kernel,
        (
            shaped((1, 1024), F32),
            shaped((1, 1024), F32),
            shaped((1, 2048), F32),
            shaped((1, 2, 512), F32),
        ),
        (payload,),
        10**5,
        core=(place.t.reshape(1).astype(jnp.int32),),
    )

    sent_two = send_plane(blocks_two, False)
    flips = ((0, 0), (0, 1), (1, 0), (1, 1))
    attend_own, forward_own, *attend_rest = call(
        last_sums_kernel,
        (shaped((32, 1024), F32), shaped((2, 16, 2048), F32), shaped((32, 1024)),
         shaped((96, 1024)), shaped((32, 1024))),
        tuple(by_step(blocks_two[0], sent_two)),
        10**6,
        far=(row_payload, grad_ada, ada_bias_sum),
    )
    (moved,) = pack(
        [block_low, grad_stream.astype(BF16)], [[(0, 0, 128), (1, 0, 128)]], (attend_own,)
    )
    moved = swap_layout(moved).reshape(2, 128, 1024)
    block_output, grad_latents = moved[:1], moved[1:]
    flipped_t, flipped_w, flipped_both = (
        flip_x(item, w, t) for item, (w, t) in zip(attend_rest, flips[1:])
    )
    forward_other = flipped_w[32:].reshape(2, 2, 16, 1024).transpose(0, 2, 1, 3)
    forward_grads = forward_own + forward_other.reshape(2, 16, 2048).astype(F32)
    reduced = add_up(attend_own, [flipped_t, flipped_w[:32], flipped_both]).reshape(2, 16, 1024)
    mine = lax.dynamic_index_in_dim(reduced, place.c, 0, keepdims=False)
    theirs = swap_core(lax.dynamic_index_in_dim(reduced, 1 - place.c, 0, keepdims=False))
    low = jnp.where(place.first, mine, theirs).reshape(16, 4, 256)
    high = jnp.where(place.first, theirs, mine).reshape(16, 4, 256)
    reduced = jnp.concatenate([low, high], axis=2)


    return (
        block_output,
        grad_latents,
        grad_conditioning,
        grad_ada,
        ada_bias_sum,
        reduced[None, :, :3],
        attend_bias_sum,
        reduced[None, :, 3],
        project_bias_sum,
        forward_grads[0][None],
        hidden_bias_sum,
        forward_grads[1][None],
        out_bias_sum,
    )


def solution(mesh):
    fine = Mesh(mesh.devices.reshape(4, 2, 4, 2, 2), ("z", "w", "y", "c", "t"))
    return jax.shard_map(
        shards,
        mesh=fine,
        in_specs=(
            P(DP, "t", None),
            P(DP, None),
            P(DP, "t", None),
            P(DP, None, None),
            P(),
            P(None, DP, None, "t"),
            P(None, None, "t"),
            P(None, DP, "t"),
            P(),
            P(None, DP, "t"),
            P(None, "t"),
            P(None, DP, "t"),
            P(),
        ),
        out_specs=(
            P(DP, "t", None),
            P(DP, "t", None),
            P(DP, None),
            P(DP, None, None),
            P(),
            P(None, DP, None, "t"),
            P(None, None, "t"),
            P(None, DP, "t"),
            P(),
            P(None, DP, "t"),
            P(None, "t"),
            P(None, DP, "t"),
            P(),
        ),
        check_vma=False,
    )
```
